32 devices in a mesh: node: 8 (over z, x), head: 4 (over y, core).
Axes of the slice: x: 2, y: 2, z: 4, core: 2. Of those that a mesh axis runs over, the one named last changes fastest.
Arguments:
- queries: bfloat16 [768, 8192], P('head', 'node'), may hold values from -9 to 9
- key_rows: bfloat16 [768, 8192], P('head', 'node'), may hold values from -9 to 9
- value_rows: bfloat16 [768, 8192], P('head', 'node'), may hold values from -6 to 6
- out_weight: bfloat16 [768, 768], P('head'), may hold values from -0.21875 to 0.21875
- cotangent: bfloat16 [768, 8192], P('head', 'node'), may hold values from -12 to 12
- cluster_ids: int32 [8192], P('node'), may hold values from 0 to 15, as said below
- members: int32 [16, 1024], P('node'), may hold values from 0 to 8191, as said below
- counts: int32 [16], P('node'), may hold values from 0 to 1024, as said below
Outputs:
- output: bfloat16 [768, 8192], P('head', 'node')
- grad_queries: bfloat16 [768, 8192], P('head', 'node')
- grad_keys: bfloat16 [768, 8192], P('head', 'node')
- grad_values: bfloat16 [768, 8192], P('head', 'node')
The draws below stay inside these ranges and needn't reach their ends.
Inputs may be any that keep to these rules, and one draw needn't show every extreme that they name: Node i is listed exactly once, in cluster cluster_ids[i]; cluster c is owned by index c // 2 of node. Each index of node has 256 of its nodes in clusters of a quarter of the owners (one of them takes 256 from every index), 128 in clusters of half of the owners, and none in the rest. Row c lists the members of cluster c in its first counts[c] entries; the other entries are arbitrary node ids. `counts`: each owner's members fill its clusters 1024 at a time: all of its clusters but at most one are full or empty.
All inputs are finite; a program needn't handle non-finite values.
Results may differ from the reference program's by a relative error of at most 0.012.
The reference program's roundings to bfloat16 on the way count: a program that leaves them out, or rounds other values in their place, can miss the bound.
Values may be sent and summed in bfloat16 or wider, within the bound.
No kernel may reach another device: no remote copies, remote signals or barrier semaphores. Data moves between devices by JAX's collectives and lax.ppermute only.
A program may use at most 128 MiB of HBM per device.

```python
import math
import jax
import jax.numpy as jnp
from jax import lax

HEADS = 12
HEAD_DIM = 64
D = 768
CLUSTER = 1024
CLU_DEV = 2
NODE_DEV = 1024
NODES = 8192
CLUSTERS = 16
N_NODE = 8


def cluster_graph(key):
    hot_key, order_key, place_key, sort_key, label_key, filler_key = jax.random.split(key, 6)
    owners = N_NODE
    depth = 2 * NODE_DEV // N_NODE
    hot = jax.random.randint(hot_key, (), 0, owners)
    column = jnp.arange(owners, dtype=jnp.int32)
    owner_scores = jax.random.randint(order_key, (owners, owners), 0, (1 << 30) // owners) * owners + column[None, :]
    owner_scores = jnp.where(column[None, :] == hot, -1, owner_scores)
    ranking = jnp.argsort(jnp.argsort(owner_scores, axis=1), axis=1)
    sent = jnp.where(ranking < owners // 4, depth, jnp.where(ranking < 3 * owners // 4, depth // 2, 0)).astype(jnp.int32)
    ends = jnp.cumsum(sent, axis=1)
    local = jnp.arange(NODE_DEV, dtype=jnp.int32)
    place_scores = jax.random.randint(place_key, (owners, NODE_DEV), 0, (1 << 30) // NODE_DEV) * NODE_DEV + local[None, :]
    position = jnp.argsort(jnp.argsort(place_scores, axis=1), axis=1)
    node_owner = jnp.sum(position[:, :, None] >= ends[:, None, :], axis=2).astype(jnp.int32).reshape(-1)
    shuffle = jax.random.permutation(sort_key, NODES).astype(jnp.int32)
    order = jnp.argsort(node_owner * NODES + shuffle)
    spot = jnp.argsort(order).astype(jnp.int32)
    load = jnp.sum(sent, axis=0)
    start = jnp.cumsum(load) - load
    rank_in_owner = spot - start[node_owner]
    local_cluster = rank_in_owner // CLUSTER
    slot = rank_in_owner % CLUSTER
    label_scores = jax.random.randint(label_key, (owners, CLU_DEV), 0, (1 << 30) // CLU_DEV) * CLU_DEV + jnp.arange(CLU_DEV, dtype=jnp.int32)[None, :]
    labels = jnp.argsort(label_scores, axis=1).astype(jnp.int32)
    cluster = (node_owner * CLU_DEV + labels[node_owner, local_cluster]).astype(jnp.int32)
    filler = jax.random.randint(filler_key, (CLUSTERS, CLUSTER), 0, NODES).astype(jnp.int32)
    members = filler.at[cluster, slot].set(jnp.arange(NODES, dtype=jnp.int32))
    counts = jnp.zeros((CLUSTERS,), jnp.int32).at[cluster].add(1)
    return (cluster, members, counts)


def draw_queries(key, part):
    key = jax.random.fold_in(key, 11)
    rows = jnp.clip(1.5 * jax.random.normal(key, (NODES, D), jnp.float32), -9.0, 9.0)
    return rows.T.astype(jnp.bfloat16)


def draw_key_rows(key, part):
    key = jax.random.fold_in(key, 12)
    rows = jnp.clip(1.5 * jax.random.normal(key, (NODES, D), jnp.float32), -9.0, 9.0)
    return rows.T.astype(jnp.bfloat16)


def draw_cluster_ids(key, part):
    return cluster_graph(key)[0]


def draw_members(key, part):
    return cluster_graph(key)[1]


def draw_counts(key, part):
    return cluster_graph(key)[2]


def block_levels(stream_key, extent, pieces, smallest, top_value):
    loudness = 1.0
    for dim, blocks in pieces:
        heights = jax.random.uniform(jax.random.fold_in(jax.random.fold_in(stream_key, 6), dim), (blocks,), jnp.float32, smallest / len(pieces), top_value / len(pieces))
        loudness = loudness * jnp.repeat(jnp.exp(heights), extent[dim] // blocks).reshape((-1,) + (1,) * (len(extent) - 1 - dim))
    return loudness


def scatter_about(rng, dims, width, bound, cuts=(), kind=jnp.bfloat16):
    array = jax.random.normal(rng, dims, jnp.float32) * width
    if len(cuts) > 0:
        array = block_levels(rng, dims, cuts, -0.22, 0.18) * array
    return jnp.clip(array, min=-bound, max=bound).astype(kind)


def setup_inputs(seed: int = 0) -> dict:
    streams_of = jax.random.split(jax.random.key(seed), 9)
    queries = draw_queries(jax.random.fold_in(streams_of[8], 71), 0)
    key_rows = draw_key_rows(jax.random.fold_in(streams_of[8], 71), 0)
    value_rows = scatter_about(streams_of[2], (D, NODES), 1.0, 6.0, ((0, 4), (1, 8)))
    out_weight = scatter_about(streams_of[3], (D, D), D ** -0.5, 0.21875, ((0, 4),))
    cotangent = scatter_about(streams_of[4], (D, NODES), 2.0, 12.0, ((0, 4), (1, 8)))
    cluster_ids = draw_cluster_ids(jax.random.fold_in(streams_of[8], 71), 0)
    members = draw_members(jax.random.fold_in(streams_of[8], 71), 0)
    counts = draw_counts(jax.random.fold_in(streams_of[8], 71), 0)
    return dict(queries=queries, key_rows=key_rows, value_rows=value_rows, out_weight=out_weight, cotangent=cotangent, cluster_ids=cluster_ids, members=members, counts=counts)


masked_score = -1e+30

def attend(query_part, key_part, value_part, grad_part, count):
    wide = jnp.float32
    valid = jnp.arange(CLUSTER) < count
    scale = 1.0 / math.sqrt(HEAD_DIM)
    scores = jnp.einsum('qhe,khe->hqk', query_part.astype(wide), key_part.astype(wide)) * scale
    scores = jnp.where(valid[None, None, :], scores, masked_score)
    raised = jnp.exp(scores - lax.optimization_barrier(jnp.max(scores, axis=2, keepdims=True)))
    weights = raised / lax.optimization_barrier(jnp.sum(raised, axis=2, keepdims=True))
    weights = jnp.where(valid[None, :, None], weights, 0.0)
    narrow = lax.optimization_barrier(weights.astype(jnp.bfloat16))
    spread = narrow.astype(wide)
    mixed = jnp.einsum('hqk,khe->qhe', spread, value_part.astype(wide)).astype(jnp.bfloat16)
    mixed = lax.optimization_barrier(mixed)
    dweights = jnp.einsum('qhe,khe->hqk', grad_part.astype(wide), value_part.astype(wide))
    delta = jnp.einsum('qhe,qhe->hq', grad_part.astype(wide), mixed.astype(wide))
    dscores = lax.optimization_barrier((spread * (dweights - delta[:, :, None])).astype(jnp.bfloat16))
    dscores = dscores.astype(wide)
    grad_query = (jnp.einsum('hqk,khe->qhe', dscores, key_part.astype(wide)) * scale).astype(jnp.bfloat16)
    grad_key = (jnp.einsum('hqk,qhe->khe', dscores, query_part.astype(wide)) * scale).astype(jnp.bfloat16)
    grad_value = jnp.einsum('hqk,qhe->khe', spread, grad_part.astype(wide)).astype(jnp.bfloat16)
    return (mixed, grad_query, grad_key, grad_value)

def reference(queries, key_rows, value_rows, out_weight, cotangent, cluster_ids, members, counts):
    query_nodes = queries.T
    key_nodes = key_rows.T
    value_nodes = value_rows.T
    grad_in = jnp.dot(cotangent.T, out_weight.T, preferred_element_type=jnp.float32).astype(jnp.bfloat16)

    def one_cluster(pair):
        listed, count = pair

        def pick(table):
            return table[listed].reshape(CLUSTER, HEADS, HEAD_DIM)

        def work():
            parts = attend(pick(query_nodes), pick(key_nodes), pick(value_nodes), pick(grad_in), count)
            return tuple((part.reshape(CLUSTER, D) for part in parts))

        def spare():
            return tuple((jnp.zeros((CLUSTER, D), jnp.bfloat16) for index in range(4)))
        return lax.cond(count > 0, work, spare)
    results = lax.map(one_cluster, (members, counts))
    valid = jnp.arange(CLUSTER)[None, :] < counts[:, None]
    target = jnp.where(valid, members, NODES).reshape(-1).astype(jnp.int32)
    slots = jnp.broadcast_to(jnp.arange(CLUSTER, dtype=jnp.int32)[None, :], (CLUSTERS, CLUSTER)).reshape(-1)
    position = jnp.zeros((NODES,), jnp.int32).at[target].set(slots, mode='drop')
    flat_index = (cluster_ids * CLUSTER + position).astype(jnp.int32)
    attention, grad_queries, grad_keys, grad_values = (part.reshape(-1, D)[flat_index] for part in results)
    output = jnp.dot(attention, out_weight, preferred_element_type=jnp.float32).astype(jnp.bfloat16)
    return (output.T, grad_queries.T, grad_keys.T, grad_values.T)
```

```python
import functools
import math

import jax
import jax.numpy as jnp
from jax import lax
from jax.experimental import pallas as pl
from jax.experimental.pallas import tpu as pltpu
from jax.sharding import PartitionSpec as P

HEAD_DIM = 64
CLUSTER = 1024
PAIR = 2 * HEAD_DIM
TILE = 256
SPARE = 32
VMEM_LIMIT = 56 * 1024 * 1024
masked_score = -1e30

NT = (((1,), (1,)), ((), ()))
NN = (((1,), (0,)), ((), ()))


def dot(left, right, dims=NN):
    return lax.dot_general(left, right, dims, preferred_element_type=jnp.float32)


class Plan:
    def __init__(self, nodes, rows, width, clusters):
        self.nodes = nodes
        self.rows = rows
        self.width = width
        self.heads = width // HEAD_DIM
        self.clusters = clusters
        self.total = nodes * clusters
        self.depth = 2 * rows // nodes
        self.half = self.depth // 2
        large = min(self.heads, nodes // 4)
        self.cap = large * self.depth + (self.heads - large) * self.half
        self.shift = tuple(3 * head % nodes for head in range(self.heads))
        self.units = self.heads * clusters
        self.tiles = self.units * (CLUSTER // TILE)


def owner_rows(plan, hist, owner):
    return sum(hist[owner * plan.clusters + index] for index in range(plan.clusters))


def each_chunk(plan, hist, starts, visit):
    def begin(owner, at):
        starts[owner] = at
        return at + owner_rows(plan, hist, owner) // plan.half

    lax.fori_loop(0, plan.nodes, begin, jnp.int32(0))

    def block(dest, carry):
        slot = jnp.int32(0)
        for head in range(plan.heads):
            owner = lax.rem(dest + plan.shift[head], plan.nodes)
            row = starts[owner]
            count = owner_rows(plan, hist, owner) // plan.half
            for index in range(2):

                @pl.when(index < count)
                def _(slot=slot, head=head, row=row, index=index):
                    visit(dest, slot + index, head, row + index)

            slot = slot + count
        return carry

    lax.fori_loop(0, plan.nodes, block, 0)


def chunk_rows(plan, index):
    return pl.ds(pl.multiple_of(index * plan.half, plan.half), plan.half)


def spread(plan, pos, first, second, hist, starts, ordered, wire):
    parts = []
    for head in range(plan.heads):
        span = slice(head * HEAD_DIM, (head + 1) * HEAD_DIM)
        parts += [first[span, :], second[span, :]]
    source = jnp.concatenate(parts, axis=0)
    for at in range(0, plan.rows, TILE):
        row = lax.broadcasted_iota(jnp.int32, (TILE, plan.rows), 0) + at
        pick = (row == pos).astype(jnp.bfloat16)
        ordered[at : at + TILE, :] = dot(pick, source, NT).astype(jnp.bfloat16)
    wire[...] = jnp.zeros_like(wire)

    def visit(dest, slot, head, row):
        wire[dest, chunk_rows(plan, slot), :] = ordered[
            chunk_rows(plan, row), head * PAIR : (head + 1) * PAIR
        ]

    each_chunk(plan, hist, starts, visit)


def pack_first_kernel(plan, hist, ids, queries, keys, wire, pos_out, starts, ordered):
    rows = plan.rows
    rank = ids[...] * rows + lax.broadcasted_iota(jnp.int32, (1, rows), 1)
    rank = rank.astype(jnp.float32)
    column = jnp.broadcast_to(rank, (128, rows)).T
    parts = []
    for at in range(0, rows, 128):
        below = (column < rank[:, at : at + 128]).astype(jnp.float32)
        parts.append(jnp.sum(below, axis=0, keepdims=True))
    pos = jnp.concatenate(parts, axis=1).astype(jnp.int32)
    pos_out[...] = pos
    spread(plan, pos, queries[...], keys[...], hist, starts, ordered, wire)


def pack_second_kernel(plan, hist, pos, values, weight, cotangent, wire, starts, ordered):
    grad_in = dot(weight[...], cotangent[...]).astype(jnp.bfloat16)
    spread(plan, pos[...], values[...], grad_in, hist, starts, ordered, wire)


def unpack_kernel(plan, hist, pos, wire, first, second, starts, ordered):
    def visit(dest, slot, head, row):
        ordered[head, chunk_rows(plan, row), :] = wire[dest, chunk_rows(plan, slot), :]

    each_chunk(plan, hist, starts, visit)
    source = jnp.concatenate(
        [ordered[head].astype(jnp.float32).T.astype(jnp.bfloat16) for head in range(plan.heads)],
        axis=0,
    )
    for at in range(0, plan.rows, TILE):
        row = lax.broadcasted_iota(jnp.int32, (plan.rows, TILE), 0)
        pick = (row == pos[:, at : at + TILE]).astype(jnp.bfloat16)
        out = dot(source, pick).astype(jnp.bfloat16)
        for head in range(plan.heads):
            span = slice(head * HEAD_DIM, (head + 1) * HEAD_DIM)
            first[span, at : at + TILE] = out[head * PAIR : head * PAIR + HEAD_DIM, :]
            second[span, at : at + TILE] = out[head * PAIR + HEAD_DIM : (head + 1) * PAIR, :]


def each_group(plan, hist, me, visit):
    def source(index, places):
        at = index * plan.cap
        after = []
        for head in range(plan.heads):
            owner = lax.rem(me + plan.shift[head], plan.nodes)
            for cluster in range(plan.clusters):
                unit = head * plan.clusters + cluster
                count = hist[index * plan.total + owner * plan.clusters + cluster]
                visit(unit, places[unit], at, count)
                at = at + count
                after.append(places[unit] + count)
        return tuple(after)

    return lax.fori_loop(0, plan.nodes, source, (jnp.int32(0),) * plan.units)


def gather_units(plan, hist, me, wire, stage, held, counts):
    flat = plan.nodes * plan.cap
    for index in range(plan.nodes):
        stage[index * plan.cap : (index + 1) * plan.cap, :] = wire[index].astype(jnp.float32)
    stage[flat : flat + SPARE, :] = jnp.zeros((SPARE, PAIR), jnp.float32)

    def visit(unit, place, at, count):
        def step(index, carry):
            held[unit, pl.ds(place + index * SPARE, SPARE), :] = stage[
                pl.ds(at + index * SPARE, SPARE), :
            ]
            return carry

        lax.fori_loop(0, pl.cdiv(count, SPARE), step, 0)

    totals = each_group(plan, hist, me, visit)
    for unit in range(plan.units):
        counts[unit] = totals[unit]


def scatter_units(plan, hist, me, held, stage, wire):
    def visit(unit, place, at, count):
        def step(index, carry):
            stage[pl.ds(at + index * SPARE, SPARE), :] = held[
                unit, pl.ds(place + index * SPARE, SPARE), :
            ]
            return carry

        lax.fori_loop(0, pl.cdiv(count, SPARE), step, 0)

    each_group(plan, hist, me, visit)
    for index in range(plan.nodes):
        wire[index] = stage[index * plan.cap : (index + 1) * plan.cap, :].astype(jnp.bfloat16)


def unit_rows(held, unit, count):
    row = lax.broadcasted_iota(jnp.int32, (CLUSTER, PAIR), 0)
    return jnp.where(row < count, held[unit, 0:CLUSTER, :], 0.0)


def weights_kernel(plan, hist, me, wire, queries, keys_t, weights, stage, held, counts, query_aug,
                   key_aug, out, sems):
    gather_units(plan, hist, me[0], wire, stage, held, counts)
    factor = math.log2(math.e) / math.sqrt(HEAD_DIM)
    lane = lax.broadcasted_iota(jnp.int32, (CLUSTER, PAIR), 1)
    row = lax.broadcasted_iota(jnp.int32, (CLUSTER, PAIR), 0)

    def copy_out(step):
        slot = lax.rem(step, 2)
        return pltpu.make_async_copy(out.at[slot], weights.at[step], sems.at[slot])

    def one_unit(unit, step):
        count = counts[unit]
        both = unit_rows(held, unit, count)
        turned = pltpu.roll(both, HEAD_DIM, 1)
        queries[unit] = jnp.where(lane < HEAD_DIM, both, 0.0).astype(jnp.bfloat16)
        keys_t[unit] = turned.T[0:HEAD_DIM, :].astype(jnp.bfloat16)
        one = jnp.where(lane == HEAD_DIM, 1.0, 0.0)
        query_aug[...] = jnp.where(lane < HEAD_DIM, both, one).astype(jnp.bfloat16)
        outside = jnp.where(jnp.logical_and(lane == HEAD_DIM, row >= count), masked_score, 0.0)
        key_aug[...] = jnp.where(lane < HEAD_DIM, turned, outside).astype(jnp.bfloat16)

        def one_tile(tile, step):
            slot = lax.rem(step, 2)
            part = query_aug[pl.ds(pl.multiple_of(tile * TILE, TILE), TILE), :]
            scores = dot(key_aug[...], part, NT)
            raised = jnp.exp2((scores - jnp.max(scores, axis=0, keepdims=True)) * factor)
            share = 1.0 / jnp.sum(raised, axis=0, keepdims=True)

            @pl.when(step >= 2)
            def _():
                copy_out(step - 2).wait()

            out[slot] = (raised * share).astype(jnp.bfloat16)
            copy_out(step).start()
            return step + 1

        return lax.fori_loop(0, pl.cdiv(count, TILE), one_tile, step)

    steps = lax.fori_loop(0, plan.units, one_unit, jnp.int32(0))
    for back in (2, 1):

        @pl.when(steps >= back)
        def _(back=back):
            copy_out(steps - back).wait()


def grads_kernel(plan, hist, me, wire, queries, keys_t, weights, wire_first, wire_second, stage,
                 held, counts, value_turned, grad_rows, both_t, held_first, held_second, total,
                 tiles, sems):
    gather_units(plan, hist, me[0], wire, stage, held, counts)
    scale = 1.0 / math.sqrt(HEAD_DIM)
    lane = lax.broadcasted_iota(jnp.int32, (CLUSTER, PAIR), 1)
    steps = sum(pl.cdiv(counts[unit], TILE) for unit in range(plan.units))

    def copy_in(step):
        slot = lax.rem(step, 2)
        return pltpu.make_async_copy(weights.at[step], tiles.at[slot], sems.at[slot])

    @pl.when(steps > 0)
    def _():
        copy_in(0).start()

    def one_unit(unit, step):
        count = counts[unit]
        both = unit_rows(held, unit, count)
        turned = pltpu.roll(both, HEAD_DIM, 1)
        value_turned[...] = jnp.where(lane >= HEAD_DIM, turned, 0.0).astype(jnp.bfloat16)
        grad_rows[...] = jnp.where(lane >= HEAD_DIM, both, 0.0).astype(jnp.bfloat16)
        both_t[...] = both.T.astype(jnp.bfloat16)
        total[...] = jnp.zeros_like(total)

        def one_tile(tile, step):
            slot = lax.rem(step, 2)
            span = pl.ds(pl.multiple_of(tile * TILE, TILE), TILE)

            @pl.when(step + 1 < steps)
            def _():
                copy_in(step + 1).start()

            copy_in(step).wait()
            held_weights = tiles[slot]
            mixed = dot(both_t[0:HEAD_DIM, :], held_weights).astype(jnp.bfloat16)
            mixed = mixed.astype(jnp.float32)
            grad_t = both_t[HEAD_DIM:PAIR, span].astype(jnp.float32)
            delta = jnp.sum(grad_t * mixed, axis=0, keepdims=True)
            grad_part = grad_rows[span, :]
            dweights = dot(value_turned[...], grad_part, NT)
            dscores = (held_weights.astype(jnp.float32) * (dweights - delta)).astype(jnp.bfloat16)
            grad_query = dot(keys_t[unit], dscores) * scale
            held_first[unit, span, :] = jnp.concatenate([mixed, grad_query], axis=0).T
            total[...] += dot(
                jnp.concatenate([dscores, held_weights], axis=1),
                jnp.concatenate([queries[unit, span, :], grad_part], axis=0),
            )
            return step + 1

        step = lax.fori_loop(0, pl.cdiv(count, TILE), one_tile, step)
        factor = jnp.where(lane < HEAD_DIM, scale, 1.0)
        held_second[unit, 0:CLUSTER, :] = total[...] * factor
        return step

    lax.fori_loop(0, plan.units, one_unit, jnp.int32(0))
    scatter_units(plan, hist, me[0], held_first, stage, wire_first)
    scatter_units(plan, hist, me[0], held_second, stage, wire_second)


SCALARS = pl.BlockSpec(memory_space=pltpu.SMEM)
WHOLE = pl.BlockSpec(memory_space=pltpu.VMEM)
APART = pl.BlockSpec(memory_space=pl.ANY)


def call(kernel, plan, name, outs, out_specs, in_specs, scratch, flops, args):
    shapes = [jax.ShapeDtypeStruct(shape, dtype) for shape, dtype in outs]
    moved = sum(math.prod(shape) * jnp.dtype(dtype).itemsize for shape, dtype in outs)
    return pl.pallas_call(
        functools.partial(kernel, plan),
        out_shape=shapes,
        in_specs=in_specs,
        out_specs=out_specs,
        scratch_shapes=scratch,
        compiler_params=pltpu.CompilerParams(vmem_limit_bytes=VMEM_LIMIT),
        cost_estimate=pl.CostEstimate(flops=flops, bytes_accessed=2 * moved, transcendentals=0),
        name=name,
    )(*args)


def body(queries, key_rows, value_rows, out_weight, cotangent, cluster_ids, members, counts):
    nodes = lax.axis_size("node")
    width, rows = queries.shape
    plan = Plan(nodes, rows, width, members.shape[0])
    me = lax.axis_index("node").astype(jnp.int32).reshape(1)
    narrow = jnp.bfloat16
    wire_shape = ((plan.nodes, plan.cap, PAIR), narrow)
    home_shape = ((width, rows), narrow)
    starts = pltpu.SMEM((plan.nodes,), jnp.int32)
    ordered = pltpu.VMEM((rows, plan.heads * PAIR), narrow)
    stage = pltpu.VMEM((plan.nodes * plan.cap + SPARE, PAIR), jnp.float32)
    held = pltpu.VMEM((plan.units, CLUSTER + SPARE, PAIR), jnp.float32)
    unit_counts = pltpu.SMEM((plan.units,), jnp.int32)
    unit_block = pltpu.VMEM((CLUSTER, PAIR), narrow)
    tiles = pltpu.VMEM((2, CLUSTER, TILE), narrow)
    sems = pltpu.SemaphoreType.DMA((2,))

    def swap(wire):
        return lax.all_to_all(wire, "node", split_axis=0, concat_axis=0, tiled=True)

    named = jnp.arange(plan.total, dtype=jnp.int32)[:, None] == cluster_ids[None, :]
    hist = jnp.sum(named, axis=1, dtype=jnp.int32)
    all_hist = lax.all_gather(hist, "node", axis=0, tiled=True)
    all_cotangent = lax.all_gather(cotangent, "head", axis=0, tiled=True)
    all_weight = lax.all_gather(out_weight, "head", axis=0, tiled=True)

    wire, pos = call(
        pack_first_kernel, plan, "pack_queries_keys", [wire_shape, ((1, rows), jnp.int32)],
        [WHOLE, WHOLE], [SCALARS, WHOLE, WHOLE, WHOLE], [starts, ordered], 2 * 10**9,
        (hist, cluster_ids.reshape(1, rows), queries, key_rows),
    )
    query_wire = swap(wire)
    (wire,) = call(
        pack_second_kernel, plan, "pack_values_grads", [wire_shape],
        [WHOLE], [SCALARS, WHOLE, WHOLE, WHOLE, WHOLE], [starts, ordered], 2 * 10**9,
        (hist, pos, value_rows, out_weight, all_cotangent),
    )
    value_wire = swap(wire)

    unit_queries = ((plan.units, CLUSTER, PAIR), narrow)
    unit_keys = ((plan.units, HEAD_DIM, CLUSTER), narrow)
    unit_weights = ((plan.tiles, CLUSTER, TILE), narrow)
    kept_queries, kept_keys, weights = call(
        weights_kernel, plan, "weights", [unit_queries, unit_keys, unit_weights],
        [WHOLE, WHOLE, APART], [SCALARS, SCALARS, WHOLE],
        [stage, held, unit_counts, unit_block, unit_block, tiles, sems], 10 * 10**9,
        (all_hist, me, query_wire),
    )
    wire_first, wire_second = call(
        grads_kernel, plan, "attention_and_grads", [wire_shape, wire_shape],
        [WHOLE, WHOLE], [SCALARS, SCALARS, WHOLE, WHOLE, WHOLE, APART],
        [stage, held, unit_counts, unit_block, unit_block, pltpu.VMEM((PAIR, CLUSTER), narrow),
         held, held, pltpu.VMEM((CLUSTER, PAIR), jnp.float32), tiles, sems], 10 * 10**9,
        (all_hist, me, value_wire, kept_queries, kept_keys, weights),
    )

    def unpack(wire, name):
        return call(
            unpack_kernel, plan, name, [home_shape, home_shape], [WHOLE, WHOLE],
            [SCALARS, WHOLE, WHOLE],
            [starts, pltpu.VMEM((plan.heads, rows, PAIR), narrow)], 2 * 10**9,
            (hist, pos, wire),
        )

    attention, grad_queries = unpack(swap(wire_first), "unpack_attention_grad_queries")
    grad_keys, grad_values = unpack(swap(wire_second), "unpack_grad_keys_grad_values")
    all_attention = lax.all_gather(attention, "head", axis=0, tiled=True)
    mine = lax.dynamic_slice_in_dim(all_weight, lax.axis_index("head") * width, width, 1)
    output = lax.dot_general(
        mine, all_attention, (((0,), (0,)), ((), ())), preferred_element_type=jnp.float32
    ).astype(narrow)
    return (output, grad_queries, grad_keys, grad_values)


def solution(mesh):
    placed = (
        P("head", "node"),
        P("head", "node"),
        P("head", "node"),
        P("head", None),
        P("head", "node"),
        P("node"),
        P("node", None),
        P("node"),
    )
    return jax.shard_map(
        body,
        mesh=mesh,
        in_specs=placed,
        out_specs=(P("head", "node"), P("head", "node"), P("head", "node"), P("head", "node")),
        check_vma=False,
    )
```

```python
import functools
import math

import jax
import jax.numpy as jnp
from jax import lax
from jax.experimental import pallas as pl
from jax.experimental.pallas import tpu as pltpu
from jax.sharding import PartitionSpec as P

HEAD_DIM = 64
CLUSTER = 1024
PAIR = 2 * HEAD_DIM
TILE = 256
SPARE = 32
NOTE = 16
VMEM_LIMIT = 56 * 1024 * 1024
masked_score = -1e30

NT = (((1,), (1,)), ((), ()))
NN = (((1,), (0,)), ((), ()))


def dot(left, right, dims=NN):
    return lax.dot_general(left, right, dims, preferred_element_type=jnp.float32)


class Plan:
    def __init__(self, nodes, rows, width, clusters):
        self.nodes = nodes
        self.rows = rows
        self.width = width
        self.heads = width // HEAD_DIM
        self.clusters = clusters
        self.total = nodes * clusters
        self.depth = 2 * rows // nodes
        self.half = self.depth // 2
        large = min(self.heads, nodes // 4)
        self.cap = large * self.depth + (self.heads - large) * self.half
        self.shift = tuple(3 * head % nodes for head in range(self.heads))
        self.units = self.heads * clusters
        self.tiles = self.units * (CLUSTER // TILE)
        self.split = nodes <= 16 and nodes & (nodes - 1) == 0
        self.blocks = nodes if self.split else 1


def owner_rows(plan, hist, owner):
    return sum(hist[owner * plan.clusters + index] for index in range(plan.clusters))


def each_block(plan, visit):
    if plan.split:
        for index in range(plan.nodes):
            visit(index)
    else:
        lax.fori_loop(0, plan.nodes, lambda index, carry: visit(index) or carry, 0)


def block_of(plan, blocks, index):
    return blocks[index] if plan.split else blocks[0].at[index]


def partner(plan, me, index):
    return jnp.bitwise_xor(me, index) if plan.split else index


def each_chunk(plan, hist, me, starts, visit):
    def begin(owner, at):
        starts[owner] = at
        return at + owner_rows(plan, hist, owner) // plan.half

    lax.fori_loop(0, plan.nodes, begin, jnp.int32(0))

    def block(number):
        dest = partner(plan, me, number)
        slot = jnp.int32(0)
        for head in range(plan.heads):
            owner = lax.rem(dest + plan.shift[head], plan.nodes)
            row = starts[owner]
            count = owner_rows(plan, hist, owner) // plan.half
            for index in range(2):

                @pl.when(index < count)
                def _(slot=slot, head=head, row=row, index=index):
                    visit(number, slot + index, head, row + index)

            slot = slot + count

    each_block(plan, block)


def chunk_rows(plan, index):
    return pl.ds(pl.multiple_of(index * plan.half, plan.half), plan.half)


def spread(plan, pos, first, second, hist, me, starts, ordered, wires):
    parts = []
    for head in range(plan.heads):
        span = slice(head * HEAD_DIM, (head + 1) * HEAD_DIM)
        parts += [first[span, :], second[span, :]]
    source = jnp.concatenate(parts, axis=0)
    for at in range(0, plan.rows, TILE):
        row = lax.broadcasted_iota(jnp.int32, (TILE, plan.rows), 0) + at
        pick = (row == pos).astype(jnp.bfloat16)
        ordered[at : at + TILE, :] = dot(pick, source, NT).astype(jnp.bfloat16)

    def clear(number):
        block = block_of(plan, wires, number)
        block[...] = jnp.zeros(block.shape, block.dtype)

    each_block(plan, clear)

    def visit(number, slot, head, row):
        block_of(plan, wires, number)[chunk_rows(plan, slot), :] = ordered[
            chunk_rows(plan, row), head * PAIR : (head + 1) * PAIR
        ]

    each_chunk(plan, hist, me, starts, visit)


def pack_first_kernel(plan, hist, me, ids, queries, keys, *refs):
    wires, (pos_out, starts, ordered) = refs[: plan.blocks], refs[plan.blocks :]
    rows = plan.rows
    rank = ids[...] * rows + lax.broadcasted_iota(jnp.int32, (1, rows), 1)
    rank = rank.astype(jnp.float32)
    column = jnp.broadcast_to(rank, (128, rows)).T
    parts = []
    for at in range(0, rows, 128):
        below = (column < rank[:, at : at + 128]).astype(jnp.float32)
        parts.append(jnp.sum(below, axis=0, keepdims=True))
    pos = jnp.concatenate(parts, axis=1).astype(jnp.int32)
    pos_out[...] = pos
    spread(plan, pos, queries[...], keys[...], hist, me[0], starts, ordered, wires)
    lane = lax.broadcasted_iota(jnp.int32, (NOTE, PAIR), 1)

    def note(number):
        dest = partner(plan, me[0], number)
        counts = jnp.zeros((NOTE, PAIR), jnp.int32)
        for head in range(plan.heads):
            owner = lax.rem(dest + plan.shift[head], plan.nodes)
            for cluster in range(plan.clusters):
                unit = head * plan.clusters + cluster
                count = hist[owner * plan.clusters + cluster]
                counts = jnp.where(lane == unit, count, counts)
        block_of(plan, wires, number)[plan.cap :, :] = counts.astype(jnp.float32).astype(
            jnp.bfloat16
        )

    each_block(plan, note)


def pack_second_kernel(plan, hist, me, pos, values, weight, cotangent, *refs):
    wires, (starts, ordered) = refs[: plan.blocks], refs[plan.blocks :]
    grad_in = dot(weight[...], cotangent[...]).astype(jnp.bfloat16)
    spread(plan, pos[...], values[...], grad_in, hist, me[0], starts, ordered, wires)


def unpack_kernel(plan, hist, me, pos, *refs):
    wires, (first, second, starts, ordered) = refs[: plan.blocks], refs[plan.blocks :]

    def visit(number, slot, head, row):
        ordered[head, chunk_rows(plan, row), :] = block_of(plan, wires, number)[
            chunk_rows(plan, slot), :
        ]

    each_chunk(plan, hist, me[0], starts, visit)
    source = jnp.concatenate(
        [ordered[head].astype(jnp.float32).T.astype(jnp.bfloat16) for head in range(plan.heads)],
        axis=0,
    )
    for at in range(0, plan.rows, TILE):
        row = lax.broadcasted_iota(jnp.int32, (plan.rows, TILE), 0)
        pick = (row == pos[:, at : at + TILE]).astype(jnp.bfloat16)
        out = dot(source, pick).astype(jnp.bfloat16)
        for head in range(plan.heads):
            span = slice(head * HEAD_DIM, (head + 1) * HEAD_DIM)
            first[span, at : at + TILE] = out[head * PAIR : head * PAIR + HEAD_DIM, :]
            second[span, at : at + TILE] = out[head * PAIR + HEAD_DIM : (head + 1) * PAIR, :]


def each_group(plan, table, visit):
    def source(index, places):
        at = index * plan.cap
        after = []
        for unit in range(plan.units):
            count = table[index, unit]
            visit(unit, places[unit], at, count)
            at = at + count
            after.append(places[unit] + count)
        return tuple(after)

    return lax.fori_loop(0, plan.nodes, source, (jnp.int32(0),) * plan.units)


def stage_rows(plan, index):
    start = index * plan.cap
    return pl.ds(start if plan.split else pl.multiple_of(start, plan.half), plan.cap)


def gather_units(plan, table, wires, stage, held, counts):
    flat = plan.nodes * plan.cap

    def widen(index):
        block = block_of(plan, wires, index)
        stage[stage_rows(plan, index), :] = block[0 : plan.cap, :].astype(jnp.float32)

    each_block(plan, widen)
    stage[flat : flat + SPARE, :] = jnp.zeros((SPARE, PAIR), jnp.float32)

    def visit(unit, place, at, count):
        def step(index, carry):
            held[unit, pl.ds(place + index * SPARE, SPARE), :] = stage[
                pl.ds(at + index * SPARE, SPARE), :
            ]
            return carry

        lax.fori_loop(0, pl.cdiv(count, SPARE), step, 0)

    totals = each_group(plan, table, visit)
    for unit in range(plan.units):
        counts[unit] = totals[unit]


def scatter_units(plan, table, held, stage, wires):
    def visit(unit, place, at, count):
        def step(index, carry):
            stage[pl.ds(at + index * SPARE, SPARE), :] = held[
                unit, pl.ds(place + index * SPARE, SPARE), :
            ]
            return carry

        lax.fori_loop(0, pl.cdiv(count, SPARE), step, 0)

    each_group(plan, table, visit)

    def narrow(index):
        block = block_of(plan, wires, index)
        block[...] = stage[stage_rows(plan, index), :].astype(jnp.bfloat16)

    each_block(plan, narrow)


def unit_rows(held, unit, count):
    row = lax.broadcasted_iota(jnp.int32, (CLUSTER, PAIR), 0)
    return jnp.where(row < count, held[unit, 0:CLUSTER, :], 0.0)


def weights_kernel(plan, *refs):
    wires, refs = refs[: plan.blocks], refs[plan.blocks :]
    (table, queries, keys_t, weights, noted, stage, held, counts, query_aug, key_aug, out, sems,
     table_sem) = refs

    def note(index):
        row = block_of(plan, wires, index)[plan.cap :, :].astype(jnp.float32)
        noted[pl.ds(index, 1), :] = row[0:1, :].astype(jnp.int32)

    each_block(plan, note)
    table_copy = pltpu.make_async_copy(noted, table, table_sem)
    table_copy.start()
    table_copy.wait()
    gather_units(plan, table, wires, stage, held, counts)
    factor = math.log2(math.e) / math.sqrt(HEAD_DIM)
    lane = lax.broadcasted_iota(jnp.int32, (CLUSTER, PAIR), 1)
    row = lax.broadcasted_iota(jnp.int32, (CLUSTER, PAIR), 0)

    def copy_out(step):
        slot = lax.rem(step, 2)
        return pltpu.make_async_copy(out.at[slot], weights.at[step], sems.at[slot])

    def one_unit(unit, step):
        count = counts[unit]
        both = unit_rows(held, unit, count)
        turned = pltpu.roll(both, HEAD_DIM, 1)
        queries[unit] = jnp.where(lane < HEAD_DIM, both, 0.0).astype(jnp.bfloat16)
        keys_t[unit] = turned.T[0:HEAD_DIM, :].astype(jnp.bfloat16)
        one = jnp.where(lane == HEAD_DIM, 1.0, 0.0)
        query_aug[...] = jnp.where(lane < HEAD_DIM, both, one).astype(jnp.bfloat16)
        outside = jnp.where(jnp.logical_and(lane == HEAD_DIM, row >= count), masked_score, 0.0)
        key_aug[...] = jnp.where(lane < HEAD_DIM, turned, outside).astype(jnp.bfloat16)

        def one_tile(tile, step):
            slot = lax.rem(step, 2)
            part = query_aug[pl.ds(pl.multiple_of(tile * TILE, TILE), TILE), :]
            scores = dot(key_aug[...], part, NT)
            raised = jnp.exp2((scores - jnp.max(scores, axis=0, keepdims=True)) * factor)
            share = 1.0 / jnp.sum(raised, axis=0, keepdims=True)

            @pl.when(step >= 2)
            def _():
                copy_out(step - 2).wait()

            out[slot] = (raised * share).astype(jnp.bfloat16)
            copy_out(step).start()
            return step + 1

        return lax.fori_loop(0, pl.cdiv(count, TILE), one_tile, step)

    steps = lax.fori_loop(0, plan.units, one_unit, jnp.int32(0))
    for back in (2, 1):

        @pl.when(steps >= back)
        def _(back=back):
            copy_out(steps - back).wait()


def queries_kernel(plan, table, *refs):
    wires, refs = refs[: plan.blocks], refs[plan.blocks :]
    keys_t, weights = refs[:2]
    wires_out, refs = refs[2 : 2 + plan.blocks], refs[2 + plan.blocks :]
    (dscores_out, grads, counts_out, stage, held, counts, value_turned, both_t, held_out, tiles,
     out, sems, out_sems) = refs
    gather_units(plan, table, wires, stage, held, counts)
    scale = 1.0 / math.sqrt(HEAD_DIM)
    lane = lax.broadcasted_iota(jnp.int32, (CLUSTER, PAIR), 1)
    steps = jnp.int32(0)
    for unit in range(plan.units):
        steps = steps + pl.cdiv(counts[unit], TILE)
        counts_out[unit] = counts[unit]

    def copy_in(step):
        slot = lax.rem(step, 2)
        return pltpu.make_async_copy(weights.at[step], tiles.at[slot], sems.at[slot])

    def copy_out(step):
        slot = lax.rem(step, 2)
        return pltpu.make_async_copy(out.at[slot], dscores_out.at[step], out_sems.at[slot])

    @pl.when(steps > 0)
    def _():
        copy_in(0).start()

    def one_unit(unit, step):
        count = counts[unit]
        both = unit_rows(held, unit, count)
        turned = pltpu.roll(both, HEAD_DIM, 1)
        value_turned[...] = jnp.where(lane >= HEAD_DIM, turned, 0.0).astype(jnp.bfloat16)
        grads[unit] = jnp.where(lane >= HEAD_DIM, both, 0.0).astype(jnp.bfloat16)
        both_t[...] = both.T.astype(jnp.bfloat16)

        def one_tile(tile, step):
            slot = lax.rem(step, 2)
            span = pl.ds(pl.multiple_of(tile * TILE, TILE), TILE)

            @pl.when(step + 1 < steps)
            def _():
                copy_in(step + 1).start()

            copy_in(step).wait()
            held_weights = tiles[slot]
            mixed = dot(both_t[0:HEAD_DIM, :], held_weights).astype(jnp.bfloat16)
            mixed = mixed.astype(jnp.float32)
            grad_t = both_t[HEAD_DIM:PAIR, span].astype(jnp.float32)
            delta = jnp.sum(grad_t * mixed, axis=0, keepdims=True)
            dweights = dot(value_turned[...], grads[unit, span, :], NT)
            dscores = (held_weights.astype(jnp.float32) * (dweights - delta)).astype(jnp.bfloat16)

            @pl.when(step >= 2)
            def _():
                copy_out(step - 2).wait()

            out[slot] = dscores
            copy_out(step).start()
            grad_query = dot(keys_t[unit], dscores) * scale
            held_out[unit, span, :] = jnp.concatenate([mixed, grad_query], axis=0).T
            return step + 1

        return lax.fori_loop(0, pl.cdiv(count, TILE), one_tile, step)

    lax.fori_loop(0, plan.units, one_unit, jnp.int32(0))
    scatter_units(plan, table, held_out, stage, wires_out)
    for back in (2, 1):

        @pl.when(steps >= back)
        def _(back=back):
            copy_out(steps - back).wait()


def keys_kernel(plan, table, counts, queries, grads, weights, dscores, *refs):
    wires_out, refs = refs[: plan.blocks], refs[plan.blocks :]
    stage, held_out, total, tiles, sems = refs
    scale = 1.0 / math.sqrt(HEAD_DIM)
    lane = lax.broadcasted_iota(jnp.int32, (CLUSTER, PAIR), 1)
    steps = jnp.int32(0)
    for unit in range(plan.units):
        steps = steps + pl.cdiv(counts[unit], TILE)

    def copies_in(step):
        slot = lax.rem(step, 2)
        return [
            pltpu.make_async_copy(
                source.at[step],
                tiles.at[slot, :, pl.ds(index * TILE, TILE)],
                sems.at[slot, index],
            )
            for index, source in enumerate((dscores, weights))
        ]

    @pl.when(steps > 0)
    def _():
        for copy in copies_in(0):
            copy.start()

    def one_unit(unit, step):
        total[...] = jnp.zeros_like(total)

        def one_tile(tile, step):
            slot = lax.rem(step, 2)
            span = pl.ds(pl.multiple_of(tile * TILE, TILE), TILE)

            @pl.when(step + 1 < steps)
            def _():
                for copy in copies_in(step + 1):
                    copy.start()

            for copy in copies_in(step):
                copy.wait()
            total[...] += dot(
                tiles[slot],
                jnp.concatenate([queries[unit, span, :], grads[unit, span, :]], axis=0),
            )
            return step + 1

        step = lax.fori_loop(0, pl.cdiv(counts[unit], TILE), one_tile, step)
        factor = jnp.where(lane < HEAD_DIM, scale, 1.0)
        held_out[unit, 0:CLUSTER, :] = total[...] * factor
        return step

    lax.fori_loop(0, plan.units, one_unit, jnp.int32(0))
    scatter_units(plan, table, held_out, stage, wires_out)


SCALARS = pl.BlockSpec(memory_space=pltpu.SMEM)
WHOLE = pl.BlockSpec(memory_space=pltpu.VMEM)
APART = pl.BlockSpec(memory_space=pl.ANY)


def call(kernel, plan, name, outs, out_specs, in_specs, scratch, flops, args):
    shapes = [jax.ShapeDtypeStruct(shape, dtype) for shape, dtype in outs]
    moved = sum(math.prod(shape) * jnp.dtype(dtype).itemsize for shape, dtype in outs)
    return pl.pallas_call(
        functools.partial(kernel, plan),
        out_shape=shapes,
        in_specs=in_specs,
        out_specs=out_specs,
        scratch_shapes=scratch,
        compiler_params=pltpu.CompilerParams(vmem_limit_bytes=VMEM_LIMIT),
        cost_estimate=pl.CostEstimate(flops=flops, bytes_accessed=2 * moved, transcendentals=0),
        name=name,
    )(*args)


def body(queries, key_rows, value_rows, out_weight, cotangent, cluster_ids, members, counts):
    nodes = lax.axis_size("node")
    width, rows = queries.shape
    plan = Plan(nodes, rows, width, members.shape[0])
    me = lax.axis_index("node").astype(jnp.int32).reshape(1)
    narrow = jnp.bfloat16
    home_shape = ((width, rows), narrow)
    starts = pltpu.SMEM((plan.nodes,), jnp.int32)
    ordered = pltpu.VMEM((rows, plan.heads * PAIR), narrow)
    stage = pltpu.VMEM((plan.nodes * plan.cap + SPARE, PAIR), jnp.float32)
    held = pltpu.VMEM((plan.units, CLUSTER + SPARE, PAIR), jnp.float32)
    unit_counts = pltpu.SMEM((plan.units,), jnp.int32)
    unit_block = pltpu.VMEM((CLUSTER, PAIR), narrow)
    tiles = pltpu.VMEM((2, CLUSTER, TILE), narrow)
    sems = pltpu.SemaphoreType.DMA((2,))
    lead = () if plan.split else (plan.nodes,)
    wire_shapes = [(lead + (plan.cap, PAIR), narrow)] * plan.blocks
    noted_shapes = [(lead + (plan.cap + NOTE, PAIR), narrow)] * plan.blocks
    wire_specs = [WHOLE] * plan.blocks

    def swap(wires):
        if not plan.split:
            return [lax.all_to_all(wires[0], "node", split_axis=0, concat_axis=0, tiled=True)]
        arrived = list(wires)
        for index in range(plan.nodes - 1, 0, -1):
            pairs = [(node, node ^ index) for node in range(plan.nodes)]
            arrived[index] = lax.ppermute(wires[index], "node", pairs)
        return arrived

    named = jnp.arange(plan.total, dtype=jnp.int32)[:, None] == cluster_ids[None, :]
    hist = jnp.sum(named, axis=1, dtype=jnp.int32)
    all_cotangent = lax.all_gather(cotangent, "head", axis=0, tiled=True)
    all_weight = lax.all_gather(out_weight, "head", axis=0, tiled=True)

    *wires, pos = call(
        pack_first_kernel, plan, "pack_queries_keys",
        noted_shapes + [((1, rows), jnp.int32)], wire_specs + [WHOLE],
        [SCALARS, SCALARS, WHOLE, WHOLE, WHOLE], [starts, ordered], 2 * 10**9,
        (hist, me, cluster_ids.reshape(1, rows), queries, key_rows),
    )
    query_wires = swap(wires)
    wires = call(
        pack_second_kernel, plan, "pack_values_grads", wire_shapes, wire_specs,
        [SCALARS, SCALARS, WHOLE, WHOLE, WHOLE, WHOLE], [starts, ordered], 2 * 10**9,
        (hist, me, pos, value_rows, out_weight, all_cotangent),
    )
    value_wires = swap(wires)

    unit_rows_shape = ((plan.units, CLUSTER, PAIR), narrow)
    unit_keys_shape = ((plan.units, HEAD_DIM, CLUSTER), narrow)
    tiles_shape = ((plan.tiles, CLUSTER, TILE), narrow)
    table_shape = (plan.nodes, PAIR)
    table, kept_queries, kept_keys, weights = call(
        weights_kernel, plan, "weights",
        [(table_shape, jnp.int32), unit_rows_shape, unit_keys_shape, tiles_shape],
        [SCALARS, WHOLE, WHOLE, APART], wire_specs,
        [pltpu.VMEM(table_shape, jnp.int32), stage, held, unit_counts, unit_block, unit_block,
         tiles, sems, pltpu.SemaphoreType.DMA], 10 * 10**9,
        query_wires,
    )
    *first_wires, dscores, kept_grads, counted = call(
        queries_kernel, plan, "attention_and_grad_queries",
        wire_shapes + [tiles_shape, unit_rows_shape, ((plan.units,), jnp.int32)],
        wire_specs + [APART, WHOLE, SCALARS], [SCALARS] + wire_specs + [WHOLE, APART],
        [stage, held, unit_counts, unit_block, pltpu.VMEM((PAIR, CLUSTER), narrow), held, tiles,
         tiles, sems, sems], 10 * 10**9,
        [table] + value_wires + [kept_keys, weights],
    )
    second_wires = call(
        keys_kernel, plan, "grad_keys_and_grad_values", wire_shapes, wire_specs,
        [SCALARS, SCALARS, WHOLE, WHOLE, APART, APART],
        [stage, held, pltpu.VMEM((CLUSTER, PAIR), jnp.float32),
         pltpu.VMEM((2, CLUSTER, 2 * TILE), narrow), pltpu.SemaphoreType.DMA((2, 2))], 10 * 10**9,
        [table, counted, kept_queries, kept_grads, weights, dscores],
    )

    def unpack(wires, name):
        return call(
            unpack_kernel, plan, name, [home_shape, home_shape], [WHOLE, WHOLE],
            [SCALARS, SCALARS, WHOLE] + wire_specs,
            [starts, pltpu.VMEM((plan.heads, rows, PAIR), narrow)], 2 * 10**9,
            [hist, me, pos] + wires,
        )

    attention, grad_queries = unpack(swap(first_wires), "unpack_attention_grad_queries")
    grad_keys, grad_values = unpack(swap(second_wires), "unpack_grad_keys_grad_values")
    all_attention = lax.all_gather(attention, "head", axis=0, tiled=True)
    mine = lax.dynamic_slice_in_dim(all_weight, lax.axis_index("head") * width, width, 1)
    output = lax.dot_general(
        mine, all_attention, (((0,), (0,)), ((), ())), preferred_element_type=jnp.float32
    ).astype(narrow)
    return (output, grad_queries, grad_keys, grad_values)


def solution(mesh):
    placed = (
        P("head", "node"),
        P("head", "node"),
        P("head", "node"),
        P("head", None),
        P("head", "node"),
        P("node"),
        P("node", None),
        P("node"),
    )
    return jax.shard_map(
        body,
        mesh=mesh,
        in_specs=placed,
        out_specs=(P("head", "node"), P("head", "node"), P("head", "node"), P("head", "node")),
        check_vma=False,
    )
```

```python
import functools
import math

import jax
import jax.numpy as jnp
from jax import lax
from jax.experimental import pallas as pl
from jax.experimental.pallas import tpu as pltpu
from jax.sharding import PartitionSpec as P

HEAD_DIM = 64
CLUSTER = 1024
PAIR = 2 * HEAD_DIM
TILE = 256
SPARE = 32
NOTE = 16
MASKS = (
    (7, 6, 5, 4, 3, 2, 1),
    (5, 4, 3, 2, 1, 7, 6),
    (2, 1, 7, 6, 5, 4, 3),
    (1, 7, 6, 5, 4, 3, 2),
)
VMEM_LIMIT = 56 * 1024 * 1024
masked_score = -1e30

NT = (((1,), (1,)), ((), ()))
NN = (((1,), (0,)), ((), ()))


def dot(left, right, dims=NN):
    return lax.dot_general(left, right, dims, preferred_element_type=jnp.float32)


class Plan:
    def __init__(self, nodes, rows, width, clusters, masks):
        self.nodes = nodes
        self.rows = rows
        self.width = width
        self.heads = width // HEAD_DIM
        self.clusters = clusters
        self.total = nodes * clusters
        self.depth = 2 * rows // nodes
        self.half = self.depth // 2
        large = min(self.heads, nodes // 4)
        self.cap = large * self.depth + (self.heads - large) * self.half
        self.shift = tuple(3 * head % nodes for head in range(self.heads))
        self.units = self.heads * clusters
        self.tiles = self.units * (CLUSTER // TILE)
        self.split = nodes == len(masks) + 1
        self.masks = (0,) + masks
        self.blocks = nodes if self.split else 1


def owner_rows(plan, hist, owner):
    return sum(hist[owner * plan.clusters + index] for index in range(plan.clusters))


def each_block(plan, visit):
    if plan.split:
        for index in range(plan.nodes):
            visit(index)
    else:
        lax.fori_loop(0, plan.nodes, lambda index, carry: visit(index) or carry, 0)


def block_of(plan, blocks, index):
    return blocks[index] if plan.split else blocks[0].at[index]


def partner(plan, me, index):
    return jnp.bitwise_xor(me, plan.masks[index]) if plan.split else index


def each_chunk(plan, hist, me, starts, visit):
    def begin(owner, at):
        starts[owner] = at
        return at + owner_rows(plan, hist, owner) // plan.half

    lax.fori_loop(0, plan.nodes, begin, jnp.int32(0))

    def block(number):
        dest = partner(plan, me, number)
        slot = jnp.int32(0)
        for head in range(plan.heads):
            owner = lax.rem(dest + plan.shift[head], plan.nodes)
            row = starts[owner]
            count = owner_rows(plan, hist, owner) // plan.half
            for index in range(2):

                @pl.when(index < count)
                def _(slot=slot, head=head, row=row, index=index):
                    visit(number, slot + index, head, row + index)

            slot = slot + count

    each_block(plan, block)


def chunk_rows(plan, index):
    return pl.ds(pl.multiple_of(index * plan.half, plan.half), plan.half)


def spread(plan, pos, first, second, hist, me, starts, ordered, wires):
    parts = []
    for head in range(plan.heads):
        span = slice(head * HEAD_DIM, (head + 1) * HEAD_DIM)
        parts += [first[span, :], second[span, :]]
    source = jnp.concatenate(parts, axis=0)
    for at in range(0, plan.rows, TILE):
        row = lax.broadcasted_iota(jnp.int32, (TILE, plan.rows), 0) + at
        pick = (row == pos).astype(jnp.bfloat16)
        ordered[at : at + TILE, :] = dot(pick, source, NT).astype(jnp.bfloat16)

    def clear(number):
        block = block_of(plan, wires, number)
        block[...] = jnp.zeros(block.shape, block.dtype)

    each_block(plan, clear)

    def visit(number, slot, head, row):
        block_of(plan, wires, number)[chunk_rows(plan, slot), :] = ordered[
            chunk_rows(plan, row), head * PAIR : (head + 1) * PAIR
        ]

    each_chunk(plan, hist, me, starts, visit)


def pack_first_kernel(plan, hist, me, ids, queries, keys, *refs):
    wires, (pos_out, starts, ordered) = refs[: plan.blocks], refs[plan.blocks :]
    rows = plan.rows
    rank = ids[...] * rows + lax.broadcasted_iota(jnp.int32, (1, rows), 1)
    rank = rank.astype(jnp.float32)
    column = jnp.broadcast_to(rank, (128, rows)).T
    parts = []
    for at in range(0, rows, 128):
        below = (column < rank[:, at : at + 128]).astype(jnp.float32)
        parts.append(jnp.sum(below, axis=0, keepdims=True))
    pos = jnp.concatenate(parts, axis=1).astype(jnp.int32)
    pos_out[...] = pos
    spread(plan, pos, queries[...], keys[...], hist, me[0], starts, ordered, wires)
    lane = lax.broadcasted_iota(jnp.int32, (NOTE, PAIR), 1)

    def note(number):
        dest = partner(plan, me[0], number)
        counts = jnp.zeros((NOTE, PAIR), jnp.int32)
        for head in range(plan.heads):
            owner = lax.rem(dest + plan.shift[head], plan.nodes)
            for cluster in range(plan.clusters):
                unit = head * plan.clusters + cluster
                count = hist[owner * plan.clusters + cluster]
                counts = jnp.where(lane == unit, count, counts)
        block_of(plan, wires, number)[plan.cap :, :] = counts.astype(jnp.float32).astype(
            jnp.bfloat16
        )

    each_block(plan, note)


def pack_second_kernel(plan, hist, me, pos, values, weight, cotangent, *refs):
    wires, (starts, ordered) = refs[: plan.blocks], refs[plan.blocks :]
    grad_in = dot(weight[...], cotangent[...]).astype(jnp.bfloat16)
    spread(plan, pos[...], values[...], grad_in, hist, me[0], starts, ordered, wires)


def unpack_kernel(plan, hist, me, pos, *refs):
    wires, (first, second, starts, ordered) = refs[: plan.blocks], refs[plan.blocks :]

    def visit(number, slot, head, row):
        ordered[head, chunk_rows(plan, row), :] = block_of(plan, wires, number)[
            chunk_rows(plan, slot), :
        ]

    each_chunk(plan, hist, me[0], starts, visit)
    source = jnp.concatenate(
        [ordered[head].astype(jnp.float32).T.astype(jnp.bfloat16) for head in range(plan.heads)],
        axis=0,
    )
    for at in range(0, plan.rows, TILE):
        row = lax.broadcasted_iota(jnp.int32, (plan.rows, TILE), 0)
        pick = (row == pos[:, at : at + TILE]).astype(jnp.bfloat16)
        out = dot(source, pick).astype(jnp.bfloat16)
        for head in range(plan.heads):
            span = slice(head * HEAD_DIM, (head + 1) * HEAD_DIM)
            first[span, at : at + TILE] = out[head * PAIR : head * PAIR + HEAD_DIM, :]
            second[span, at : at + TILE] = out[head * PAIR + HEAD_DIM : (head + 1) * PAIR, :]


def each_group(plan, table, visit):
    def source(line, block, places):
        at = block * (plan.cap + SPARE)
        after = []
        for unit in range(plan.units):
            count = table[line, unit]
            visit(unit, places[unit], at, count)
            at = at + count
            after.append(places[unit] + count)
        return tuple(after)

    places = (jnp.int32(0),) * plan.units
    if not plan.split:
        return lax.fori_loop(0, plan.nodes, lambda at, places: source(at, at, places), places)
    for mask in range(plan.nodes):
        places = source(mask, plan.masks.index(mask), places)
    return places


def stage_rows(plan, index):
    start = index * (plan.cap + SPARE)
    return pl.ds(start if plan.split else pl.multiple_of(start, plan.half), plan.cap)


def gather_units(plan, table, wires, stage, held, counts):
    def widen(index):
        block = block_of(plan, wires, index)
        stage[stage_rows(plan, index), :] = block[0 : plan.cap, :].astype(jnp.float32)

    each_block(plan, widen)

    def visit(unit, place, at, count):
        def step(index, carry):
            held[unit, pl.ds(place + index * SPARE, SPARE), :] = stage[
                pl.ds(at + index * SPARE, SPARE), :
            ]
            return carry

        lax.fori_loop(0, pl.cdiv(count, SPARE), step, 0)

    totals = each_group(plan, table, visit)
    for unit in range(plan.units):
        counts[unit] = totals[unit]


def scatter_units(plan, table, held, stage, wires):
    def visit(unit, place, at, count):
        def step(index, carry):
            stage[pl.ds(at + index * SPARE, SPARE), :] = held[
                unit, pl.ds(place + index * SPARE, SPARE), :
            ]
            return carry

        lax.fori_loop(0, pl.cdiv(count, SPARE), step, 0)

    each_group(plan, table, visit)

    def narrow(index):
        block = block_of(plan, wires, index)
        block[...] = stage[stage_rows(plan, index), :].astype(jnp.bfloat16)

    each_block(plan, narrow)


def unit_rows(held, unit, count):
    row = lax.broadcasted_iota(jnp.int32, (CLUSTER, PAIR), 0)
    return jnp.where(row < count, held[unit, 0:CLUSTER, :], 0.0)


def weights_kernel(plan, *refs):
    wires, refs = refs[: plan.blocks], refs[plan.blocks :]
    (table, queries, keys_t, weights, noted, stage, held, counts, query_aug, key_aug, out, sems,
     table_sem) = refs

    def note(index):
        row = block_of(plan, wires, index)[plan.cap :, :].astype(jnp.float32)
        line = plan.masks[index] if plan.split else index
        noted[pl.ds(line, 1), :] = row[0:1, :].astype(jnp.int32)

    each_block(plan, note)
    table_copy = pltpu.make_async_copy(noted, table, table_sem)
    table_copy.start()
    table_copy.wait()
    gather_units(plan, table, wires, stage, held, counts)
    factor = math.log2(math.e) / math.sqrt(HEAD_DIM)
    lane = lax.broadcasted_iota(jnp.int32, (CLUSTER, PAIR), 1)
    row = lax.broadcasted_iota(jnp.int32, (CLUSTER, PAIR), 0)

    def copy_out(step):
        slot = lax.rem(step, 2)
        return pltpu.make_async_copy(out.at[slot], weights.at[step], sems.at[slot])

    def one_unit(unit, step):
        count = counts[unit]
        both = unit_rows(held, unit, count)
        turned = pltpu.roll(both, HEAD_DIM, 1)
        queries[unit] = jnp.where(lane < HEAD_DIM, both, 0.0).astype(jnp.bfloat16)
        keys_t[unit] = turned.T[0:HEAD_DIM, :].astype(jnp.bfloat16)
        one = jnp.where(lane == HEAD_DIM, 1.0, 0.0)
        query_aug[...] = jnp.where(lane < HEAD_DIM, both, one).astype(jnp.bfloat16)
        outside = jnp.where(jnp.logical_and(lane == HEAD_DIM, row >= count), masked_score, 0.0)
        key_aug[...] = jnp.where(lane < HEAD_DIM, turned, outside).astype(jnp.bfloat16)

        def one_tile(tile, step):
            slot = lax.rem(step, 2)
            part = query_aug[pl.ds(pl.multiple_of(tile * TILE, TILE), TILE), :]
            scores = dot(key_aug[...], part, NT)
            raised = jnp.exp2((scores - jnp.max(scores, axis=0, keepdims=True)) * factor)
            share = 1.0 / jnp.sum(raised, axis=0, keepdims=True)

            @pl.when(step >= 2)
            def _():
                copy_out(step - 2).wait()

            out[slot] = (raised * share).astype(jnp.bfloat16)
            copy_out(step).start()
            return step + 1

        return lax.fori_loop(0, pl.cdiv(count, TILE), one_tile, step)

    steps = lax.fori_loop(0, plan.units, one_unit, jnp.int32(0))
    for back in (2, 1):

        @pl.when(steps >= back)
        def _(back=back):
            copy_out(steps - back).wait()


def queries_kernel(plans, table, *refs):
    plan, plan_out = plans
    wires, refs = refs[: plan.blocks], refs[plan.blocks :]
    keys_t, weights = refs[:2]
    wires_out, refs = refs[2 : 2 + plan.blocks], refs[2 + plan.blocks :]
    (dscores_out, grads, counts_out, stage, held, counts, value_turned, both_t, held_out, tiles,
     out, sems, out_sems) = refs
    gather_units(plan, table, wires, stage, held, counts)
    scale = 1.0 / math.sqrt(HEAD_DIM)
    lane = lax.broadcasted_iota(jnp.int32, (CLUSTER, PAIR), 1)
    steps = jnp.int32(0)
    for unit in range(plan.units):
        steps = steps + pl.cdiv(counts[unit], TILE)
        counts_out[unit] = counts[unit]

    def copy_in(step):
        slot = lax.rem(step, 2)
        return pltpu.make_async_copy(weights.at[step], tiles.at[slot], sems.at[slot])

    def copy_out(step):
        slot = lax.rem(step, 2)
        return pltpu.make_async_copy(out.at[slot], dscores_out.at[step], out_sems.at[slot])

    @pl.when(steps > 0)
    def _():
        copy_in(0).start()

    def one_unit(unit, step):
        count = counts[unit]
        both = unit_rows(held, unit, count)
        turned = pltpu.roll(both, HEAD_DIM, 1)
        value_turned[...] = jnp.where(lane >= HEAD_DIM, turned, 0.0).astype(jnp.bfloat16)
        grads[unit] = jnp.where(lane >= HEAD_DIM, both, 0.0).astype(jnp.bfloat16)
        both_t[...] = both.T.astype(jnp.bfloat16)

        def one_tile(tile, step):
            slot = lax.rem(step, 2)
            span = pl.ds(pl.multiple_of(tile * TILE, TILE), TILE)

            @pl.when(step + 1 < steps)
            def _():
                copy_in(step + 1).start()

            copy_in(step).wait()
            held_weights = tiles[slot]
            mixed = dot(both_t[0:HEAD_DIM, :], held_weights).astype(jnp.bfloat16)
            mixed = mixed.astype(jnp.float32)
            grad_t = both_t[HEAD_DIM:PAIR, span].astype(jnp.float32)
            delta = jnp.sum(grad_t * mixed, axis=0, keepdims=True)
            dweights = dot(value_turned[...], grads[unit, span, :], NT)
            dscores = (held_weights.astype(jnp.float32) * (dweights - delta)).astype(jnp.bfloat16)

            @pl.when(step >= 2)
            def _():
                copy_out(step - 2).wait()

            out[slot] = dscores
            copy_out(step).start()
            grad_query = dot(keys_t[unit], dscores) * scale
            held_out[unit, span, :] = jnp.concatenate([mixed, grad_query], axis=0).T
            return step + 1

        return lax.fori_loop(0, pl.cdiv(count, TILE), one_tile, step)

    lax.fori_loop(0, plan.units, one_unit, jnp.int32(0))
    scatter_units(plan_out, table, held_out, stage, wires_out)
    for back in (2, 1):

        @pl.when(steps >= back)
        def _(back=back):
            copy_out(steps - back).wait()


def keys_kernel(plan, table, counts, queries, grads, weights, dscores, *refs):
    wires_out, refs = refs[: plan.blocks], refs[plan.blocks :]
    stage, held_out, total, tiles, sems = refs
    scale = 1.0 / math.sqrt(HEAD_DIM)
    lane = lax.broadcasted_iota(jnp.int32, (CLUSTER, PAIR), 1)
    steps = jnp.int32(0)
    for unit in range(plan.units):
        steps = steps + pl.cdiv(counts[unit], TILE)

    def copies_in(step):
        slot = lax.rem(step, 2)
        return [
            pltpu.make_async_copy(
                source.at[step],
                tiles.at[slot, :, pl.ds(index * TILE, TILE)],
                sems.at[slot, index],
            )
            for index, source in enumerate((dscores, weights))
        ]

    @pl.when(steps > 0)
    def _():
        for copy in copies_in(0):
            copy.start()

    def one_unit(unit, step):
        total[...] = jnp.zeros_like(total)

        def one_tile(tile, step):
            slot = lax.rem(step, 2)
            span = pl.ds(pl.multiple_of(tile * TILE, TILE), TILE)

            @pl.when(step + 1 < steps)
            def _():
                for copy in copies_in(step + 1):
                    copy.start()

            for copy in copies_in(step):
                copy.wait()
            total[...] += dot(
                tiles[slot],
                jnp.concatenate([queries[unit, span, :], grads[unit, span, :]], axis=0),
            )
            return step + 1

        step = lax.fori_loop(0, pl.cdiv(counts[unit], TILE), one_tile, step)
        factor = jnp.where(lane < HEAD_DIM, scale, 1.0)
        held_out[unit, 0:CLUSTER, :] = total[...] * factor
        return step

    lax.fori_loop(0, plan.units, one_unit, jnp.int32(0))
    scatter_units(plan, table, held_out, stage, wires_out)


SCALARS = pl.BlockSpec(memory_space=pltpu.SMEM)
WHOLE = pl.BlockSpec(memory_space=pltpu.VMEM)
APART = pl.BlockSpec(memory_space=pl.ANY)


def call(kernel, plan, name, outs, out_specs, in_specs, scratch, flops, args):
    shapes = [jax.ShapeDtypeStruct(shape, dtype) for shape, dtype in outs]
    moved = sum(math.prod(shape) * jnp.dtype(dtype).itemsize for shape, dtype in outs)
    return pl.pallas_call(
        functools.partial(kernel, plan),
        out_shape=shapes,
        in_specs=in_specs,
        out_specs=out_specs,
        scratch_shapes=scratch,
        compiler_params=pltpu.CompilerParams(vmem_limit_bytes=VMEM_LIMIT),
        cost_estimate=pl.CostEstimate(flops=flops, bytes_accessed=2 * moved, transcendentals=0),
        name=name,
    )(*args)


def body(queries, key_rows, value_rows, out_weight, cotangent, cluster_ids, members, counts):
    nodes = lax.axis_size("node")
    width, rows = queries.shape
    query_plan, value_plan, first_plan, second_plan = [
        Plan(nodes, rows, width, members.shape[0], masks) for masks in MASKS
    ]
    plan = query_plan
    me = lax.axis_index("node").astype(jnp.int32).reshape(1)
    narrow = jnp.bfloat16
    home_shape = ((width, rows), narrow)
    starts = pltpu.SMEM((plan.nodes,), jnp.int32)
    ordered = pltpu.VMEM((rows, plan.heads * PAIR), narrow)
    stage = pltpu.VMEM((plan.nodes * (plan.cap + SPARE), PAIR), jnp.float32)
    held = pltpu.VMEM((plan.units, CLUSTER + SPARE, PAIR), jnp.float32)
    unit_counts = pltpu.SMEM((plan.units,), jnp.int32)
    unit_block = pltpu.VMEM((CLUSTER, PAIR), narrow)
    tiles = pltpu.VMEM((2, CLUSTER, TILE), narrow)
    sems = pltpu.SemaphoreType.DMA((2,))

    def blocks(plan, extra=0):
        lead = () if plan.split else (plan.nodes,)
        return [(lead + (plan.cap + extra, PAIR), narrow)] * plan.blocks

    def specs(plan):
        return [WHOLE] * plan.blocks

    def after(value, *others):
        return lax.optimization_barrier((value,) + others)[0]

    def swap(plan, wires):
        if not plan.split:
            return [lax.all_to_all(wires[0], "node", split_axis=0, concat_axis=0, tiled=True)]
        arrived = list(wires)
        for index in range(1, plan.nodes):
            pairs = [(node, node ^ plan.masks[index]) for node in range(plan.nodes)]
            arrived[index] = lax.ppermute(wires[index], "node", pairs)
        return arrived

    named = jnp.arange(plan.total, dtype=jnp.int32)[:, None] == cluster_ids[None, :]
    hist = jnp.sum(named, axis=1, dtype=jnp.int32)
    all_cotangent = lax.all_gather(cotangent, "head", axis=0, tiled=True)
    all_weight = lax.all_gather(out_weight, "head", axis=0, tiled=True)

    *wires, pos = call(
        pack_first_kernel, plan, "pack_queries_keys",
        blocks(plan, NOTE) + [((1, rows), jnp.int32)], specs(plan) + [WHOLE],
        [SCALARS, SCALARS, WHOLE, WHOLE, WHOLE], [starts, ordered], 2 * 10**9,
        (hist, me, cluster_ids.reshape(1, rows), queries, key_rows),
    )
    query_wires = swap(plan, wires)
    wires = call(
        pack_second_kernel, value_plan, "pack_values_grads", blocks(plan), specs(plan),
        [SCALARS, SCALARS, WHOLE, WHOLE, WHOLE, WHOLE], [starts, ordered], 2 * 10**9,
        (hist, me, pos, value_rows, out_weight, all_cotangent),
    )
    value_wires = swap(value_plan, wires)
    query_wires = [after(query_wires[0], wires[0])] + query_wires[1:]

    unit_rows_shape = ((plan.units, CLUSTER, PAIR), narrow)
    unit_keys_shape = ((plan.units, HEAD_DIM, CLUSTER), narrow)
    tiles_shape = ((plan.tiles, CLUSTER, TILE), narrow)
    table_shape = (plan.nodes, PAIR)
    table, kept_queries, kept_keys, weights = call(
        weights_kernel, plan, "weights",
        [(table_shape, jnp.int32), unit_rows_shape, unit_keys_shape, tiles_shape],
        [SCALARS, WHOLE, WHOLE, APART], specs(plan),
        [pltpu.VMEM(table_shape, jnp.int32), stage, held, unit_counts, unit_block, unit_block,
         tiles, sems, pltpu.SemaphoreType.DMA], 10 * 10**9,
        query_wires,
    )
    *first_wires, dscores, kept_grads, counted = call(
        queries_kernel, (value_plan, first_plan), "attention_and_grad_queries",
        blocks(plan) + [tiles_shape, unit_rows_shape, ((plan.units,), jnp.int32)],
        specs(plan) + [APART, WHOLE, SCALARS], [SCALARS] + specs(plan) + [WHOLE, APART],
        [stage, held, unit_counts, unit_block, pltpu.VMEM((PAIR, CLUSTER), narrow), held, tiles,
         tiles, sems, sems], 10 * 10**9,
        [table] + value_wires + [kept_keys, weights],
    )
    second_wires = call(
        keys_kernel, second_plan, "grad_keys_and_grad_values", blocks(plan), specs(plan),
        [SCALARS, SCALARS, WHOLE, WHOLE, APART, APART],
        [stage, held, pltpu.VMEM((CLUSTER, PAIR), jnp.float32),
         pltpu.VMEM((2, CLUSTER, 2 * TILE), narrow), pltpu.SemaphoreType.DMA((2, 2))], 10 * 10**9,
        [table, counted, kept_queries, kept_grads, weights, dscores],
    )

    def unpack(plan, wires, name):
        return call(
            unpack_kernel, plan, name, [home_shape, home_shape], [WHOLE, WHOLE],
            [SCALARS, SCALARS, WHOLE] + specs(plan),
            [starts, pltpu.VMEM((plan.heads, rows, PAIR), narrow)], 2 * 10**9,
            [hist, me, pos] + wires,
        )

    first_back = swap(first_plan, first_wires)
    second_back = swap(second_plan, second_wires)
    first_back = [after(first_back[0], second_wires[0])] + first_back[1:]
    attention, grad_queries = unpack(first_plan, first_back, "unpack_attention_grad_queries")
    grad_keys, grad_values = unpack(second_plan, second_back, "unpack_grad_keys_grad_values")
    all_attention = lax.all_gather(attention, "head", axis=0, tiled=True)
    mine = lax.dynamic_slice_in_dim(all_weight, lax.axis_index("head") * width, width, 1)
    output = lax.dot_general(
        mine, all_attention, (((0,), (0,)), ((), ())), preferred_element_type=jnp.float32
    ).astype(narrow)
    return (output, grad_queries, grad_keys, grad_values)


def solution(mesh):
    placed = (
        P("head", "node"),
        P("head", "node"),
        P("head", "node"),
        P("head", None),
        P("head", "node"),
        P("node"),
        P("node", None),
        P("node"),
    )
    return jax.shard_map(
        body,
        mesh=mesh,
        in_specs=placed,
        out_specs=(P("head", "node"), P("head", "node"), P("head", "node"), P("head", "node")),
        check_vma=False,
    )
```

```python
import functools
import math

import jax
import jax.numpy as jnp
from jax import lax
from jax.experimental import pallas as pl
from jax.experimental.pallas import tpu as pltpu
from jax.sharding import PartitionSpec as P

HEAD_DIM = 64
CLUSTER = 1024
PAIR = 2 * HEAD_DIM
TILE = 256
SPARE = 32
NOTE = 16
HEAD_DEVICES = 4
MASKS = (
    (7, 6, 5, 4, 3, 2, 1),
    (1, 2, 7, 6, 5, 4, 3),
    (),
    (),
)
PAIRED_NODES = 8
UNIT_LIMIT = 52
SLOTS = 4
masked_score = -1e30

NT = (((1,), (1,)), ((), ()))
NN = (((1,), (0,)), ((), ()))


def dot(left, right, dims=NN):
    return lax.dot_general(left, right, dims, preferred_element_type=jnp.float32)


class Plan:
    def __init__(self, nodes, rows, width, clusters, masks):
        self.nodes = nodes
        self.rows = rows
        self.width = width
        self.heads = width // HEAD_DIM
        self.clusters = clusters
        self.total = nodes * clusters
        self.depth = 2 * rows // nodes
        self.half = self.depth // 2
        large = min(self.heads, nodes // 4)
        self.cap = large * self.depth + (self.heads - large) * self.half
        self.shift = tuple(3 * head % nodes for head in range(self.heads))
        self.units = self.heads * clusters
        self.tiles = self.units * (CLUSTER // TILE)
        self.paired = nodes == PAIRED_NODES
        self.split = self.paired and len(masks) > 0
        self.masks = (0,) + masks
        self.blocks = nodes if self.split else 1


def owner_rows(plan, hist, owner):
    return sum(hist[owner * plan.clusters + index] for index in range(plan.clusters))


def each_block(plan, visit):
    if plan.split:
        for index in range(plan.nodes):
            visit(index)
    else:
        lax.fori_loop(0, plan.nodes, lambda index, carry: (visit(index), carry)[1], 0)


def block_of(plan, blocks, index):
    return blocks[index] if plan.split else blocks[0].at[index]


def partner(plan, me, index):
    return jnp.bitwise_xor(me, plan.masks[index]) if plan.split else index


def each_chunk(plan, hist, me, starts, visit):
    def begin(owner, at):
        starts[owner] = at
        return at + owner_rows(plan, hist, owner) // plan.half

    lax.fori_loop(0, plan.nodes, begin, jnp.int32(0))

    def block(number):
        dest = partner(plan, me, number)
        slot = jnp.int32(0)
        for head in range(plan.heads):
            owner = lax.rem(dest + plan.shift[head], plan.nodes)
            row = starts[owner]
            count = owner_rows(plan, hist, owner) // plan.half
            for index in range(2):

                @pl.when(index < count)
                def _(slot=slot, head=head, row=row, index=index):
                    visit(number, slot + index, head, row + index)

            slot = slot + count

    each_block(plan, block)


def chunk_rows(plan, index):
    return pl.ds(pl.multiple_of(index * plan.half, plan.half), plan.half)


def spread(plan, pos, first, second, hist, me, starts, ordered, wires):
    parts = []
    for head in range(plan.heads):
        span = slice(head * HEAD_DIM, (head + 1) * HEAD_DIM)
        parts += [first[span, :], second[span, :]]
    source = jnp.concatenate(parts, axis=0)
    for at in range(0, plan.rows, TILE):
        row = lax.broadcasted_iota(jnp.int32, (TILE, plan.rows), 0) + at
        pick = (row == pos).astype(jnp.bfloat16)
        ordered[at : at + TILE, :] = dot(pick, source, NT).astype(jnp.bfloat16)

    def clear(number):
        block = block_of(plan, wires, number)
        block[...] = jnp.zeros(block.shape, block.dtype)

    each_block(plan, clear)

    def visit(number, slot, head, row):
        block_of(plan, wires, number)[chunk_rows(plan, slot), :] = ordered[
            chunk_rows(plan, row), head * PAIR : (head + 1) * PAIR
        ]

    each_chunk(plan, hist, me, starts, visit)


def pack_first_kernel(plan, hist, me, ids, queries, keys, *refs):
    wires, (pos_out, starts, ordered) = refs[: plan.blocks], refs[plan.blocks :]
    rows = plan.rows
    rank = ids[...] * rows + lax.broadcasted_iota(jnp.int32, (1, rows), 1)
    rank = rank.astype(jnp.float32)
    column = jnp.broadcast_to(rank, (128, rows)).T
    parts = []
    for at in range(0, rows, 128):
        below = (column < rank[:, at : at + 128]).astype(jnp.float32)
        parts.append(jnp.sum(below, axis=0, keepdims=True))
    pos = jnp.concatenate(parts, axis=1).astype(jnp.int32)
    pos_out[...] = pos
    spread(plan, pos, queries[...], keys[...], hist, me[0], starts, ordered, wires)
    lane = lax.broadcasted_iota(jnp.int32, (NOTE, PAIR), 1)

    def note(number):
        dest = partner(plan, me[0], number)
        counts = jnp.zeros((NOTE, PAIR), jnp.int32)
        for head in range(plan.heads):
            owner = lax.rem(dest + plan.shift[head], plan.nodes)
            for cluster in range(plan.clusters):
                unit = head * plan.clusters + cluster
                count = hist[owner * plan.clusters + cluster]
                counts = jnp.where(lane == unit, count, counts)
        block_of(plan, wires, number)[plan.cap :, :] = counts.astype(jnp.float32).astype(
            jnp.bfloat16
        )

    each_block(plan, note)


def pack_second_kernel(plan, hist, me, column, pos, values, weight, *refs):
    cotangents, refs = refs[:HEAD_DEVICES], refs[HEAD_DEVICES:]
    wires, (starts, ordered, gathered) = refs[: plan.blocks], refs[plan.blocks :]
    for mask in range(HEAD_DEVICES):
        place = jnp.bitwise_xor(column[0], mask) * plan.width
        span = pl.ds(pl.multiple_of(place, plan.width), plan.width)
        gathered[span, :] = cotangents[mask][...]
    grad_in = dot(weight[...], gathered[...]).astype(jnp.bfloat16)
    spread(plan, pos[...], values[...], grad_in, hist, me[0], starts, ordered, wires)


def project_kernel(plan, column, *refs):
    weights, refs = refs[:HEAD_DEVICES], refs[HEAD_DEVICES:]
    attentions, (out, piece) = refs[:HEAD_DEVICES], refs[HEAD_DEVICES:]
    for index in range(HEAD_DEVICES):

        @pl.when(column[0] == index)
        def _(index=index):
            start = index * plan.width
            for mask in range(HEAD_DEVICES):
                piece[mask] = weights[mask][:, start : start + plan.width]

    total = jnp.zeros((plan.width, plan.rows), jnp.float32)
    for mask in range(HEAD_DEVICES):
        total = total + dot(piece[mask], attentions[mask][...], (((0,), (0,)), ((), ())))
    out[...] = total.astype(jnp.bfloat16)


def unpack_kernel(plan, hist, me, pos, *refs):
    wires, (first, second, starts, ordered) = refs[: plan.blocks], refs[plan.blocks :]

    def visit(number, slot, head, row):
        ordered[head, chunk_rows(plan, row), :] = block_of(plan, wires, number)[
            chunk_rows(plan, slot), :
        ]

    each_chunk(plan, hist, me[0], starts, visit)
    source = jnp.concatenate(
        [ordered[head].astype(jnp.float32).T.astype(jnp.bfloat16) for head in range(plan.heads)],
        axis=0,
    )
    for at in range(0, plan.rows, TILE):
        row = lax.broadcasted_iota(jnp.int32, (plan.rows, TILE), 0)
        pick = (row == pos[:, at : at + TILE]).astype(jnp.bfloat16)
        out = dot(source, pick).astype(jnp.bfloat16)
        for head in range(plan.heads):
            span = slice(head * HEAD_DIM, (head + 1) * HEAD_DIM)
            first[span, at : at + TILE] = out[head * PAIR : head * PAIR + HEAD_DIM, :]
            second[span, at : at + TILE] = out[head * PAIR + HEAD_DIM : (head + 1) * PAIR, :]


def each_group(plan, table, me, visit):
    def source(line, block, places):
        at = block * (plan.cap + SPARE)
        after = []
        for unit in range(plan.units):
            count = table[line, unit]
            visit(unit, places[unit], at, count)
            at = at + count
            after.append(places[unit] + count)
        return tuple(after)

    places = (jnp.int32(0),) * plan.units
    if not plan.paired:
        return lax.fori_loop(0, plan.nodes, lambda at, places: source(at, at, places), places)
    for mask in range(plan.nodes):
        block = plan.masks.index(mask) if plan.split else jnp.bitwise_xor(me, mask)
        places = source(mask, block, places)
    return places


def stage_rows(plan, index):
    start = index * (plan.cap + SPARE)
    return pl.ds(start if plan.split else pl.multiple_of(start, NOTE), plan.cap)


def gather_units(plan, table, me, wires, stage, held, counts):
    def widen(index):
        block = block_of(plan, wires, index)
        stage[stage_rows(plan, index), :] = block[0 : plan.cap, :].astype(jnp.float32)

    each_block(plan, widen)

    def visit(unit, place, at, count):
        def step(index, carry):
            held[unit, pl.ds(place + index * SPARE, SPARE), :] = stage[
                pl.ds(at + index * SPARE, SPARE), :
            ]
            return carry

        lax.fori_loop(0, pl.cdiv(count, SPARE), step, 0)

    totals = each_group(plan, table, me, visit)
    for unit in range(plan.units):
        counts[unit] = totals[unit]


def scatter_units(plan, table, me, held, stage, wires):
    def visit(unit, place, at, count):
        def step(index, carry):
            stage[pl.ds(at + index * SPARE, SPARE), :] = held[
                unit, pl.ds(place + index * SPARE, SPARE), :
            ]
            return carry

        lax.fori_loop(0, pl.cdiv(count, SPARE), step, 0)

    each_group(plan, table, me, visit)

    def narrow(index):
        rows = stage[stage_rows(plan, index), :].astype(jnp.bfloat16)
        block_of(plan, wires, index)[...] = rows

    each_block(plan, narrow)


def unit_rows(held, unit, count):
    row = lax.broadcasted_iota(jnp.int32, (CLUSTER, PAIR), 0)
    return jnp.where(row < count, held[unit, 0:CLUSTER, :], 0.0)


def tile_steps(plan, counts):
    return sum(pl.cdiv(counts[unit], TILE) for unit in range(plan.units))


class Tiles:
    def __init__(self, array, slots, sems):
        self.array, self.slots, self.sems = array, slots, sems

    def slot(self, step):
        return lax.rem(step, SLOTS)

    def fetch(self, step):
        at = self.slot(step)
        return pltpu.make_async_copy(self.array.at[step], self.slots.at[at], self.sems.at[at])

    def begin(self, steps):
        for step in range(SLOTS - 1):

            @pl.when(step < steps)
            def _(step=step):
                self.fetch(step).start()

    def read(self, step, steps):
        @pl.when(step + SLOTS - 1 < steps)
        def _():
            self.fetch(step + SLOTS - 1).start()

        self.fetch(step).wait()
        return self.slots[self.slot(step)]

    def store(self, step):
        at = self.slot(step)
        return pltpu.make_async_copy(self.slots.at[at], self.array.at[step], self.sems.at[at])

    def write(self, step, value):
        @pl.when(step >= SLOTS)
        def _():
            self.store(step - SLOTS).wait()

        self.slots[self.slot(step)] = value
        self.store(step).start()

    def finish(self, steps):
        for back in range(SLOTS, 0, -1):

            @pl.when(steps >= back)
            def _(back=back):
                self.store(steps - back).wait()


def each_unit(plan, counts, visit):
    def one(unit, step):
        return lax.cond(counts[unit] > 0, lambda: visit(unit, step), lambda: step)

    lax.fori_loop(0, plan.units, one, jnp.int32(0))


def weights_kernel(plan, *refs):
    wires, refs = refs[: plan.blocks], refs[plan.blocks :]
    (table, queries, keys_t, weights, noted, stage, held, counts, query_aug, key_aug, table_sem,
     slots, sems) = refs
    out = Tiles(weights, slots, sems)

    def note(index):
        row = block_of(plan, wires, index)[plan.cap :, :].astype(jnp.float32)
        line = plan.masks[index] if plan.split else index
        noted[pl.ds(line, 1), :] = row[0:1, :].astype(jnp.int32)

    each_block(plan, note)
    table_copy = pltpu.make_async_copy(noted, table, table_sem)
    table_copy.start()
    table_copy.wait()
    gather_units(plan, table, None, wires, stage, held, counts)
    factor = math.log2(math.e) / math.sqrt(HEAD_DIM)
    lane = lax.broadcasted_iota(jnp.int32, (CLUSTER, PAIR), 1)
    row = lax.broadcasted_iota(jnp.int32, (CLUSTER, PAIR), 0)

    def one_unit(unit, step):
        count = counts[unit]
        both = unit_rows(held, unit, count)
        turned = pltpu.roll(both, HEAD_DIM, 1)
        queries[unit] = jnp.where(lane < HEAD_DIM, both, 0.0).astype(jnp.bfloat16)
        keys_t[unit] = turned.T[0:HEAD_DIM, :].astype(jnp.bfloat16)
        one = jnp.where(lane == HEAD_DIM, 1.0, 0.0)
        query_aug[...] = jnp.where(lane < HEAD_DIM, both, one).astype(jnp.bfloat16)
        outside = jnp.where(jnp.logical_and(lane == HEAD_DIM, row >= count), masked_score, 0.0)
        key_aug[...] = jnp.where(lane < HEAD_DIM, turned, outside).astype(jnp.bfloat16)

        def one_tile(tile, step):
            part = query_aug[pl.ds(pl.multiple_of(tile * TILE, TILE), TILE), :]
            scores = dot(key_aug[...], part, NT)
            raised = jnp.exp2((scores - jnp.max(scores, axis=0, keepdims=True)) * factor)
            share = 1.0 / jnp.sum(raised, axis=0, keepdims=True)
            out.write(step, (raised * share).astype(jnp.bfloat16))
            return step + 1

        return lax.fori_loop(0, pl.cdiv(count, TILE), one_tile, step)

    each_unit(plan, counts, one_unit)
    out.finish(tile_steps(plan, counts))


def queries_kernel(plans, table, me, *refs):
    plan, plan_out = plans
    wires, refs = refs[: plan.blocks], refs[plan.blocks :]
    keys_t, weights = refs[:2]
    wires_out, refs = refs[2 : 2 + plan_out.blocks], refs[2 + plan_out.blocks :]
    (dscores_out, grads, counts_out, stage, held, counts, value_turned, both_t, held_out,
     slots, sems, slots_out, sems_out) = refs
    tiles, out = Tiles(weights, slots, sems), Tiles(dscores_out, slots_out, sems_out)
    gather_units(plan, table, me[0], wires, stage, held, counts)
    scale = 1.0 / math.sqrt(HEAD_DIM)
    lane = lax.broadcasted_iota(jnp.int32, (CLUSTER, PAIR), 1)
    for unit in range(plan.units):
        counts_out[unit] = counts[unit]
    steps = tile_steps(plan, counts)
    tiles.begin(steps)

    def one_unit(unit, step):
        count = counts[unit]
        both = unit_rows(held, unit, count)
        turned = pltpu.roll(both, HEAD_DIM, 1)
        value_turned[...] = jnp.where(lane >= HEAD_DIM, turned, 0.0).astype(jnp.bfloat16)
        grads[unit] = jnp.where(lane >= HEAD_DIM, both, 0.0).astype(jnp.bfloat16)
        both_t[...] = both.T.astype(jnp.bfloat16)

        def one_tile(tile, step):
            span = pl.ds(pl.multiple_of(tile * TILE, TILE), TILE)
            held_weights = tiles.read(step, steps)
            mixed = dot(both_t[0:HEAD_DIM, :], held_weights).astype(jnp.bfloat16)
            mixed = mixed.astype(jnp.float32)
            grad_t = both_t[HEAD_DIM:PAIR, span].astype(jnp.float32)
            delta = jnp.sum(grad_t * mixed, axis=0, keepdims=True)
            dweights = dot(value_turned[...], grads[unit, span, :], NT)
            dscores = (held_weights.astype(jnp.float32) * (dweights - delta)).astype(jnp.bfloat16)
            out.write(step, dscores)
            grad_query = dot(keys_t[unit], dscores) * scale
            held_out[unit, span, :] = jnp.concatenate([mixed, grad_query], axis=0).T
            return step + 1

        return lax.fori_loop(0, pl.cdiv(count, TILE), one_tile, step)

    each_unit(plan, counts, one_unit)
    scatter_units(plan_out, table, me[0], held_out, stage, wires_out)
    out.finish(steps)


def keys_kernel(plan, table, me, counts, queries, grads, weights, dscores, *refs):
    wires_out, refs = refs[: plan.blocks], refs[plan.blocks :]
    stage, held_out, total, *slots, first_sems, second_sems = refs
    steps = tile_steps(plan, counts)
    tiles = Tiles(dscores, slots[0], first_sems), Tiles(weights, slots[1], second_sems)
    for source in tiles:
        source.begin(steps)
    scale = 1.0 / math.sqrt(HEAD_DIM)
    lane = lax.broadcasted_iota(jnp.int32, (CLUSTER, PAIR), 1)
    def one_unit(unit, step):
        total[...] = jnp.zeros_like(total)

        def one_tile(tile, step):
            span = pl.ds(pl.multiple_of(tile * TILE, TILE), TILE)
            total[...] += dot(
                jnp.concatenate([source.read(step, steps) for source in tiles], axis=1),
                jnp.concatenate([queries[unit, span, :], grads[unit, span, :]], axis=0),
            )
            return step + 1

        step = lax.fori_loop(0, pl.cdiv(counts[unit], TILE), one_tile, step)
        factor = jnp.where(lane < HEAD_DIM, scale, 1.0)
        held_out[unit, 0:CLUSTER, :] = total[...] * factor
        return step

    each_unit(plan, counts, one_unit)
    scatter_units(plan, table, me[0], held_out, stage, wires_out)


SCALARS = pl.BlockSpec(memory_space=pltpu.SMEM)
WHOLE = pl.BlockSpec(memory_space=pltpu.VMEM)
APART = pl.BlockSpec(memory_space=pltpu.HBM)


def call(kernel, plan, name, outs, out_specs, in_specs, scratch, flops, args, limit=56):
    shapes = [jax.ShapeDtypeStruct(shape, dtype) for shape, dtype in outs]
    moved = sum(math.prod(shape) * jnp.dtype(dtype).itemsize for shape, dtype in outs)
    return pl.pallas_call(
        functools.partial(kernel, plan),
        out_shape=shapes,
        in_specs=in_specs,
        out_specs=out_specs,
        scratch_shapes=scratch,
        compiler_params=pltpu.CompilerParams(vmem_limit_bytes=limit * 1024 * 1024),
        cost_estimate=pl.CostEstimate(flops=flops, bytes_accessed=2 * moved, transcendentals=0),
        name=name,
    )(*args)


def body(queries, key_rows, value_rows, out_weight, cotangent, cluster_ids, members, counts):
    nodes = lax.axis_size("node")
    width, rows = queries.shape
    query_plan, value_plan, first_plan, second_plan = [
        Plan(nodes, rows, width, members.shape[0], masks) for masks in MASKS
    ]
    plan = query_plan
    me = lax.axis_index("node").astype(jnp.int32).reshape(1)
    narrow = jnp.bfloat16
    home_shape = ((width, rows), narrow)
    starts = pltpu.SMEM((plan.nodes,), jnp.int32)
    ordered = pltpu.VMEM((rows, plan.heads * PAIR), narrow)
    stage = pltpu.VMEM((plan.nodes * (plan.cap + SPARE), PAIR), jnp.float32)
    held = pltpu.VMEM((plan.units, CLUSTER + SPARE, PAIR), jnp.float32)
    unit_counts = pltpu.SMEM((plan.units,), jnp.int32)
    unit_block = pltpu.VMEM((CLUSTER, PAIR), narrow)
    slots = pltpu.VMEM((SLOTS, CLUSTER, TILE), narrow)
    sems = pltpu.SemaphoreType.DMA((SLOTS,))

    def blocks(plan, extra=0):
        lead = () if plan.split else (plan.nodes,)
        return [(lead + (plan.cap + extra, PAIR), narrow)] * plan.blocks

    def specs(plan):
        return [WHOLE] * plan.blocks

    def after(value, *others):
        return lax.optimization_barrier((value,) + others)[0]

    def head_swap(value, mask):
        pairs = [(index, index ^ mask) for index in range(HEAD_DEVICES)]
        return lax.ppermute(value, "head", pairs)

    def gather_heads(value, beside=None):
        far = head_swap(value, 2)
        turned = far if beside is None else after(far, beside)
        return [value, head_swap(value, 1), far, head_swap(turned, 1)]

    def swap(plan, wires):
        if not plan.split:
            return [lax.all_to_all(wires[0], "node", split_axis=0, concat_axis=0, tiled=True)]
        arrived = list(wires)
        for index in range(1, plan.nodes):
            pairs = [(node, node ^ plan.masks[index]) for node in range(plan.nodes)]
            arrived[index] = lax.ppermute(wires[index], "node", pairs)
        return arrived

    named = jnp.arange(plan.total, dtype=jnp.int32)[:, None] == cluster_ids[None, :]
    hist = jnp.sum(named, axis=1, dtype=jnp.int32)
    column = lax.axis_index("head").astype(jnp.int32)

    cotangents = [cotangent] + [head_swap(cotangent, mask) for mask in (1, 2, 3)]
    *wires, pos = call(
        pack_first_kernel, plan, "pack_queries_keys",
        blocks(plan, NOTE) + [((1, rows), jnp.int32)], specs(plan) + [WHOLE],
        [SCALARS, SCALARS, WHOLE, WHOLE, WHOLE], [starts, ordered], 2 * 10**9,
        (hist, me, cluster_ids.reshape(1, rows), queries, key_rows),
    )
    query_wires = swap(plan, wires)
    wires = call(
        pack_second_kernel, value_plan, "pack_values_grads", blocks(value_plan), specs(value_plan),
        [SCALARS] * 3 + [WHOLE] * (3 + HEAD_DEVICES),
        [starts, ordered, pltpu.VMEM((HEAD_DEVICES * width, rows), narrow)], 2 * 10**9,
        [hist, me, column.reshape(1), pos, value_rows, out_weight] + cotangents,
    )
    value_wires = swap(value_plan, wires)
    query_wires = [after(query_wires[0], wires[0])] + query_wires[1:]

    unit_rows_shape = ((plan.units, CLUSTER, PAIR), narrow)
    unit_keys_shape = ((plan.units, HEAD_DIM, CLUSTER), narrow)
    tiles_shape = ((plan.tiles, CLUSTER, TILE), narrow)
    table_shape = (plan.nodes, PAIR)
    table, kept_queries, kept_keys, weights = call(
        weights_kernel, plan, "weights",
        [(table_shape, jnp.int32), unit_rows_shape, unit_keys_shape, tiles_shape],
        [SCALARS, WHOLE, WHOLE, APART], specs(plan),
        [pltpu.VMEM(table_shape, jnp.int32), stage, held, unit_counts, unit_block, unit_block,
         pltpu.SemaphoreType.DMA, slots, sems], 10 * 10**9,
        query_wires, UNIT_LIMIT,
    )
    all_weight = gather_heads(after(out_weight, kept_keys))
    *first_wires, dscores, kept_grads, counted = call(
        queries_kernel, (value_plan, first_plan), "attention_and_grad_queries",
        blocks(first_plan) + [tiles_shape, unit_rows_shape, ((plan.units,), jnp.int32)],
        specs(first_plan) + [APART, WHOLE, SCALARS],
        [SCALARS] * 2 + specs(value_plan) + [WHOLE, APART],
        [stage, held, unit_counts, unit_block, pltpu.VMEM((PAIR, CLUSTER), narrow), held, slots,
         sems, slots, sems], 10 * 10**9,
        [table, me] + value_wires + [kept_keys, weights], UNIT_LIMIT,
    )
    counted = after(counted, *all_weight[1:3])
    second_wires = call(
        keys_kernel, second_plan, "grad_keys_and_grad_values",
        blocks(second_plan), specs(second_plan),
        [SCALARS, SCALARS, SCALARS, WHOLE, WHOLE, APART, APART],
        [stage, held, pltpu.VMEM((CLUSTER, PAIR), jnp.float32), slots, slots, sems, sems],
        10 * 10**9,
        [table, me, counted, kept_queries, kept_grads, weights, dscores], UNIT_LIMIT,
    )

    def unpack(plan, wires, name):
        return call(
            unpack_kernel, plan, name, [home_shape, home_shape], [WHOLE, WHOLE],
            [SCALARS, SCALARS, WHOLE] + specs(plan),
            [starts, pltpu.VMEM((plan.heads, rows, PAIR), narrow)], 2 * 10**9,
            [hist, me, pos] + wires,
        )

    first_back = swap(first_plan, first_wires)
    second_back = swap(second_plan, second_wires)
    first_back = [after(first_back[0], second_wires[0])] + first_back[1:]
    attention, grad_queries = unpack(first_plan, first_back, "unpack_attention_grad_queries")
    (output,) = call(
        project_kernel, plan, "project", [home_shape], [WHOLE],
        [SCALARS] + [WHOLE] * (2 * HEAD_DEVICES),
        [pltpu.VMEM((HEAD_DEVICES, width, width), narrow)], 10**9,
        [column.reshape(1)] + all_weight + gather_heads(attention),
    )
    second_back[0] = after(second_back[0], output)
    grad_keys, grad_values = unpack(second_plan, second_back, "unpack_grad_keys_grad_values")
    return (output, grad_queries, grad_keys, grad_values)


def solution(mesh):
    placed = (
        P("head", "node"),
        P("head", "node"),
        P("head", "node"),
        P("head", None),
        P("head", "node"),
        P("node"),
        P("node", None),
        P("node"),
    )
    return jax.shard_map(
        body,
        mesh=mesh,
        in_specs=placed,
        out_specs=(P("head", "node"), P("head", "node"), P("head", "node"), P("head", "node")),
        check_vma=False,
    )
```

```python
import functools
import math

import jax
import jax.numpy as jnp
from jax import lax
from jax.experimental import pallas as pl
from jax.experimental.pallas import tpu as pltpu
from jax.sharding import PartitionSpec as P

HEAD_DIM = 64
CLUSTER = 1024
PAIR = 2 * HEAD_DIM
TILE = 256
SPARE = 32
NOTE = 16
HEAD_DEVICES = 4
MASKS = (
    (1, 7, 6, 5, 4, 2, 3),
    (1, 2, 7, 6, 5, 4, 3),
    (),
    (),
)
PAIRED_NODES = 8
UNIT_LIMIT = 46
SPACE = 16
SLOTS = 4
masked_score = -1e30

NT = (((1,), (1,)), ((), ()))
NN = (((1,), (0,)), ((), ()))
TN = (((0,), (0,)), ((), ()))


def dot(left, right, dims=NN):
    return lax.dot_general(left, right, dims, preferred_element_type=jnp.float32)


class Plan:
    def __init__(self, nodes, rows, width, clusters, masks):
        self.nodes = nodes
        self.rows = rows
        self.width = width
        self.heads = width // HEAD_DIM
        self.clusters = clusters
        self.total = nodes * clusters
        self.depth = 2 * rows // nodes
        self.half = self.depth // 2
        large = min(self.heads, nodes // 4)
        self.cap = large * self.depth + (self.heads - large) * self.half
        self.shift = tuple(3 * head % nodes for head in range(self.heads))
        self.units = self.heads * clusters
        self.tiles = self.units * (CLUSTER // TILE)
        self.paired = nodes == PAIRED_NODES
        self.split = self.paired and len(masks) > 0
        self.masks = (0,) + masks
        self.blocks = nodes if self.split else 1


def owner_rows(plan, hist, owner):
    return sum(hist[owner * plan.clusters + index] for index in range(plan.clusters))


def each_block(plan, visit):
    if plan.split:
        for index in range(plan.nodes):
            visit(index)
    else:
        lax.fori_loop(0, plan.nodes, lambda index, carry: (visit(index), carry)[1], 0)


def block_of(plan, blocks, index):
    return blocks[index] if plan.split else blocks[0].at[index]


def partner(plan, me, index):
    return jnp.bitwise_xor(me, plan.masks[index]) if plan.split else index


def each_chunk(plan, hist, me, starts, visit):
    def begin(owner, at):
        starts[owner] = at
        return at + owner_rows(plan, hist, owner) // plan.half

    lax.fori_loop(0, plan.nodes, begin, jnp.int32(0))

    def block(number):
        dest = partner(plan, me, number)
        slot = jnp.int32(0)
        for head in range(plan.heads):
            owner = lax.rem(dest + plan.shift[head], plan.nodes)
            row = starts[owner]
            count = owner_rows(plan, hist, owner) // plan.half
            for index in range(2):

                @pl.when(index < count)
                def _(slot=slot, head=head, row=row, index=index):
                    visit(number, slot + index, head, row + index)

            slot = slot + count

    each_block(plan, block)


def chunk_rows(plan, index):
    return pl.ds(pl.multiple_of(index * plan.half, plan.half), plan.half)


def spread(plan, pos, first, second, hist, me, starts, ordered, wires):
    parts = []
    for head in range(plan.heads):
        span = slice(head * HEAD_DIM, (head + 1) * HEAD_DIM)
        parts += [first[span, :], second[span, :]]
    source = jnp.concatenate(parts, axis=0)
    for at in range(0, plan.rows, TILE):
        row = lax.broadcasted_iota(jnp.int32, (TILE, plan.rows), 0) + at
        pick = (row == pos).astype(jnp.bfloat16)
        ordered[at : at + TILE, :] = dot(pick, source, NT).astype(jnp.bfloat16)

    def clear(number):
        block = block_of(plan, wires, number)
        block[...] = jnp.zeros(block.shape, block.dtype)

    each_block(plan, clear)

    def visit(number, slot, head, row):
        block_of(plan, wires, number)[chunk_rows(plan, slot), :] = ordered[
            chunk_rows(plan, row), head * PAIR : (head + 1) * PAIR
        ]

    each_chunk(plan, hist, me, starts, visit)


def pack_first_kernel(plan, hist, me, ids, queries, keys, *refs):
    wires, (pos_out, starts, ordered) = refs[: plan.blocks], refs[plan.blocks :]
    rows = plan.rows
    rank = ids[...] * rows + lax.broadcasted_iota(jnp.int32, (1, rows), 1)
    rank = rank.astype(jnp.float32)
    column = jnp.broadcast_to(rank, (128, rows)).T
    parts = []
    for at in range(0, rows, 128):
        below = (column < rank[:, at : at + 128]).astype(jnp.float32)
        parts.append(jnp.sum(below, axis=0, keepdims=True))
    pos = jnp.concatenate(parts, axis=1).astype(jnp.int32)
    pos_out[...] = pos
    spread(plan, pos, queries[...], keys[...], hist, me[0], starts, ordered, wires)
    lane = lax.broadcasted_iota(jnp.int32, (NOTE, PAIR), 1)

    def note(number):
        dest = partner(plan, me[0], number)
        counts = jnp.zeros((NOTE, PAIR), jnp.int32)
        for head in range(plan.heads):
            owner = lax.rem(dest + plan.shift[head], plan.nodes)
            for cluster in range(plan.clusters):
                unit = head * plan.clusters + cluster
                count = hist[owner * plan.clusters + cluster]
                counts = jnp.where(lane == unit, count, counts)
        block_of(plan, wires, number)[plan.cap :, :] = counts.astype(jnp.float32).astype(
            jnp.bfloat16
        )

    each_block(plan, note)


def pack_second_kernel(plan, hist, me, column, pos, values, weight, *refs):
    cotangents, refs = refs[:HEAD_DEVICES], refs[HEAD_DEVICES:]
    wires, (starts, ordered, gathered) = refs[: plan.blocks], refs[plan.blocks :]
    for mask in range(HEAD_DEVICES):
        place = jnp.bitwise_xor(column[0], mask) * plan.width
        span = pl.ds(pl.multiple_of(place, plan.width), plan.width)
        gathered[span, :] = cotangents[mask][...]
    grad_in = dot(weight[...], gathered[...]).astype(jnp.bfloat16)
    spread(plan, pos[...], values[...], grad_in, hist, me[0], starts, ordered, wires)


def project_kernel(plan, column, *refs):
    weights, refs = refs[:HEAD_DEVICES], refs[HEAD_DEVICES:]
    attentions, (out, piece) = refs[:HEAD_DEVICES], refs[HEAD_DEVICES:]
    for index in range(HEAD_DEVICES):

        @pl.when(column[0] == index)
        def _(index=index):
            start = index * plan.width
            for mask in range(HEAD_DEVICES):
                piece[mask] = weights[mask][:, start : start + plan.width]

    total = jnp.zeros((plan.width, plan.rows), jnp.float32)
    for mask in range(HEAD_DEVICES):
        total = total + dot(piece[mask], attentions[mask][...], (((0,), (0,)), ((), ())))
    out[...] = total.astype(jnp.bfloat16)


def unpack_kernel(plan, hist, me, pos, *refs):
    wires, (first, second, starts, ordered) = refs[: plan.blocks], refs[plan.blocks :]

    def visit(number, slot, head, row):
        ordered[head, chunk_rows(plan, row), :] = block_of(plan, wires, number)[
            chunk_rows(plan, slot), :
        ]

    each_chunk(plan, hist, me[0], starts, visit)
    source = jnp.concatenate([ordered[head] for head in range(plan.heads)], axis=1)
    for at in range(0, plan.rows, TILE):
        row = lax.broadcasted_iota(jnp.int32, (plan.rows, TILE), 0)
        pick = (row == pos[:, at : at + TILE]).astype(jnp.bfloat16)
        out = dot(source, pick, TN).astype(jnp.bfloat16)
        for head in range(plan.heads):
            span = slice(head * HEAD_DIM, (head + 1) * HEAD_DIM)
            first[span, at : at + TILE] = out[head * PAIR : head * PAIR + HEAD_DIM, :]
            second[span, at : at + TILE] = out[head * PAIR + HEAD_DIM : (head + 1) * PAIR, :]


def each_group(plan, table, me, visit):
    def source(line, block, places):
        at = block * (plan.cap + SPARE)
        after = []
        for unit in range(plan.units):
            count = table[line, unit]
            visit(unit, places[unit], at, count)
            at = at + count
            after.append(places[unit] + count)
        return tuple(after)

    places = (jnp.int32(0),) * plan.units
    if not plan.paired:
        return lax.fori_loop(0, plan.nodes, lambda at, places: source(at, at, places), places)
    for mask in range(plan.nodes):
        block = plan.masks.index(mask) if plan.split else jnp.bitwise_xor(me, mask)
        places = source(mask, block, places)
    return places


def stage_rows(plan, index):
    start = index * (plan.cap + SPARE)
    return pl.ds(start if plan.split else pl.multiple_of(start, NOTE), plan.cap)


def gather_units(plan, table, me, wires, stage, held, counts):
    def widen(index):
        block = block_of(plan, wires, index)
        stage[stage_rows(plan, index), :] = block[0 : plan.cap, :].astype(jnp.float32)

    each_block(plan, widen)

    def visit(unit, place, at, count):
        def step(index, carry):
            held[unit, pl.ds(place + index * SPARE, SPARE), :] = stage[
                pl.ds(at + index * SPARE, SPARE), :
            ]
            return carry

        lax.fori_loop(0, pl.cdiv(count, SPARE), step, 0)

    totals = each_group(plan, table, me, visit)
    for unit in range(plan.units):
        counts[unit] = totals[unit]


def scatter_units(plan, table, me, held, stage, wires):
    def visit(unit, place, at, count):
        def step(index, carry):
            stage[pl.ds(at + index * SPARE, SPARE), :] = held[
                unit, pl.ds(place + index * SPARE, SPARE), :
            ]
            return carry

        lax.fori_loop(0, pl.cdiv(count, SPARE), step, 0)

    each_group(plan, table, me, visit)

    def narrow(index):
        rows = stage[stage_rows(plan, index), :].astype(jnp.bfloat16)
        block_of(plan, wires, index)[...] = rows

    each_block(plan, narrow)


def unit_rows(held, unit, count):
    row = lax.broadcasted_iota(jnp.int32, (CLUSTER, PAIR), 0)
    return jnp.where(row < count, held[unit, 0:CLUSTER, :], 0.0)


def tile_steps(plan, counts):
    return sum(pl.cdiv(counts[unit], TILE) for unit in range(plan.units))


class Tiles:
    def __init__(self, array, slots, sems):
        self.array, self.slots, self.sems = array, slots, sems

    def slot(self, step):
        return lax.rem(step, SLOTS)

    def fetch(self, step):
        at = self.slot(step)
        return pltpu.make_async_copy(self.array.at[step], self.slots.at[at], self.sems.at[at])

    def begin(self, steps):
        for step in range(SLOTS - 1):

            @pl.when(step < steps)
            def _(step=step):
                self.fetch(step).start()

    def read(self, step, steps):
        @pl.when(step + SLOTS - 1 < steps)
        def _():
            self.fetch(step + SLOTS - 1).start()

        self.fetch(step).wait()
        return self.slots[self.slot(step)]

    def store(self, step):
        at = self.slot(step)
        return pltpu.make_async_copy(self.slots.at[at], self.array.at[step], self.sems.at[at])

    def write(self, step, value):
        @pl.when(step >= SLOTS)
        def _():
            self.store(step - SLOTS).wait()

        self.slots[self.slot(step)] = value
        self.store(step).start()

    def finish(self, steps):
        for back in range(SLOTS, 0, -1):

            @pl.when(steps >= back)
            def _(back=back):
                self.store(steps - back).wait()


def each_unit(plan, counts, visit):
    def one(unit, step):
        return lax.cond(counts[unit] > 0, lambda: visit(unit, step), lambda: step)

    lax.fori_loop(0, plan.units, one, jnp.int32(0))


def weights_kernel(plan, *refs):
    wires, refs = refs[: plan.blocks], refs[plan.blocks :]
    (table, queries, keys_t, weights, noted, stage, held, counts, query_aug, key_aug, table_sem,
     slots, sems) = refs
    out = Tiles(weights, slots, sems)

    def note(index):
        row = block_of(plan, wires, index)[plan.cap :, :].astype(jnp.float32)
        line = plan.masks[index] if plan.split else index
        noted[pl.ds(line, 1), :] = row[0:1, :].astype(jnp.int32)

    each_block(plan, note)
    table_copy = pltpu.make_async_copy(noted, table, table_sem)
    table_copy.start()
    table_copy.wait()
    gather_units(plan, table, None, wires, stage, held, counts)
    factor = math.log2(math.e) / math.sqrt(HEAD_DIM)
    lane = lax.broadcasted_iota(jnp.int32, (CLUSTER, PAIR), 1)
    row = lax.broadcasted_iota(jnp.int32, (CLUSTER, PAIR), 0)

    def one_unit(unit, step):
        count = counts[unit]
        both = unit_rows(held, unit, count)
        turned = pltpu.roll(both, HEAD_DIM, 1)
        queries[unit] = jnp.where(lane < HEAD_DIM, both, 0.0).astype(jnp.bfloat16)
        keys_t[unit] = turned.T[0:HEAD_DIM, :].astype(jnp.bfloat16)
        one = jnp.where(lane == HEAD_DIM, 1.0, 0.0)
        query_aug[...] = jnp.where(lane < HEAD_DIM, both, one).astype(jnp.bfloat16)
        outside = jnp.where(jnp.logical_and(lane == HEAD_DIM, row >= count), masked_score, 0.0)
        key_aug[...] = jnp.where(lane < HEAD_DIM, turned, outside).astype(jnp.bfloat16)

        def one_tile(tile, step):
            part = query_aug[pl.ds(pl.multiple_of(tile * TILE, TILE), TILE), :]
            scores = dot(key_aug[...], part, NT)
            raised = jnp.exp2((scores - jnp.max(scores, axis=0, keepdims=True)) * factor)
            share = 1.0 / jnp.sum(raised, axis=0, keepdims=True)
            out.write(step, (raised * share).astype(jnp.bfloat16))
            return step + 1

        return lax.fori_loop(0, pl.cdiv(count, TILE), one_tile, step)

    each_unit(plan, counts, one_unit)
    out.finish(tile_steps(plan, counts))


def queries_kernel(plans, table, me, *refs):
    plan, plan_out = plans
    wires, refs = refs[: plan.blocks], refs[plan.blocks :]
    keys_t, weights = refs[:2]
    wires_out, refs = refs[2 : 2 + plan_out.blocks], refs[2 + plan_out.blocks :]
    (dscores_out, grads, counts_out, stage, held, counts, value_turned, both_t, held_out,
     slots, sems, slots_out, sems_out) = refs
    tiles, out = Tiles(weights, slots, sems), Tiles(dscores_out, slots_out, sems_out)
    gather_units(plan, table, me[0], wires, stage, held, counts)
    scale = 1.0 / math.sqrt(HEAD_DIM)
    lane = lax.broadcasted_iota(jnp.int32, (CLUSTER, PAIR), 1)
    for unit in range(plan.units):
        counts_out[unit] = counts[unit]
    steps = tile_steps(plan, counts)
    tiles.begin(steps)

    def one_unit(unit, step):
        count = counts[unit]
        both = unit_rows(held, unit, count)
        turned = pltpu.roll(both, HEAD_DIM, 1)
        value_turned[...] = jnp.where(lane >= HEAD_DIM, turned, 0.0).astype(jnp.bfloat16)
        grads[unit] = jnp.where(lane >= HEAD_DIM, both, 0.0).astype(jnp.bfloat16)
        both_t[...] = both.T.astype(jnp.bfloat16)

        def one_tile(tile, step):
            span = pl.ds(pl.multiple_of(tile * TILE, TILE), TILE)
            held_weights = tiles.read(step, steps)
            mixed = dot(both_t[0:HEAD_DIM, :], held_weights).astype(jnp.bfloat16)
            mixed = mixed.astype(jnp.float32)
            grad_t = both_t[HEAD_DIM:PAIR, span].astype(jnp.float32)
            delta = jnp.sum(grad_t * mixed, axis=0, keepdims=True)
            dweights = dot(value_turned[...], grads[unit, span, :], NT)
            dscores = (held_weights.astype(jnp.float32) * (dweights - delta)).astype(jnp.bfloat16)
            out.write(step, dscores)
            grad_query = dot(keys_t[unit], dscores) * scale
            held_out[unit, span, :] = jnp.concatenate([mixed, grad_query], axis=0).T
            return step + 1

        return lax.fori_loop(0, pl.cdiv(count, TILE), one_tile, step)

    each_unit(plan, counts, one_unit)
    scatter_units(plan_out, table, me[0], held_out, stage, wires_out)
    out.finish(steps)


def keys_kernel(plan, table, me, counts, queries, grads, weights, dscores, *refs):
    wires_out, refs = refs[: plan.blocks], refs[plan.blocks :]
    stage, held_out, total, *slots, first_sems, second_sems = refs
    steps = tile_steps(plan, counts)
    tiles = Tiles(dscores, slots[0], first_sems), Tiles(weights, slots[1], second_sems)
    for source in tiles:
        source.begin(steps)
    scale = 1.0 / math.sqrt(HEAD_DIM)
    lane = lax.broadcasted_iota(jnp.int32, (CLUSTER, PAIR), 1)
    def one_unit(unit, step):
        total[...] = jnp.zeros_like(total)

        def one_tile(tile, step):
            span = pl.ds(pl.multiple_of(tile * TILE, TILE), TILE)
            total[...] += dot(
                jnp.concatenate([source.read(step, steps) for source in tiles], axis=1),
                jnp.concatenate([queries[unit, span, :], grads[unit, span, :]], axis=0),
            )
            return step + 1

        step = lax.fori_loop(0, pl.cdiv(counts[unit], TILE), one_tile, step)
        factor = jnp.where(lane < HEAD_DIM, scale, 1.0)
        held_out[unit, 0:CLUSTER, :] = total[...] * factor
        return step

    each_unit(plan, counts, one_unit)
    scatter_units(plan, table, me[0], held_out, stage, wires_out)


SCALARS = pl.BlockSpec(memory_space=pltpu.SMEM)
WHOLE = pl.BlockSpec(memory_space=pltpu.VMEM)
APART = pl.BlockSpec(memory_space=pltpu.HBM)


def call(kernel, plan, name, outs, out_specs, in_specs, scratch, flops, args, limit=56):
    shapes = [jax.ShapeDtypeStruct(shape, dtype) for shape, dtype in outs]
    moved = sum(math.prod(shape) * jnp.dtype(dtype).itemsize for shape, dtype in outs)
    return pl.pallas_call(
        functools.partial(kernel, plan),
        out_shape=shapes,
        in_specs=in_specs,
        out_specs=out_specs,
        scratch_shapes=scratch,
        compiler_params=pltpu.CompilerParams(vmem_limit_bytes=limit * 1024 * 1024),
        cost_estimate=pl.CostEstimate(flops=flops, bytes_accessed=2 * moved, transcendentals=0),
        name=name,
    )(*args)


def body(queries, key_rows, value_rows, out_weight, cotangent, cluster_ids, members, counts):
    nodes = lax.axis_size("node")
    width, rows = queries.shape
    query_plan, value_plan, first_plan, second_plan = [
        Plan(nodes, rows, width, members.shape[0], masks) for masks in MASKS
    ]
    plan = query_plan
    me = lax.axis_index("node").astype(jnp.int32).reshape(1)
    narrow = jnp.bfloat16
    home_shape = ((width, rows), narrow)
    starts = pltpu.SMEM((plan.nodes,), jnp.int32)
    ordered = pltpu.VMEM((rows, plan.heads * PAIR), narrow)
    stage = pltpu.VMEM((plan.nodes * (plan.cap + SPARE), PAIR), jnp.float32)
    held = pltpu.VMEM((plan.units, CLUSTER + SPARE, PAIR), jnp.float32)
    unit_counts = pltpu.SMEM((plan.units,), jnp.int32)
    unit_block = pltpu.VMEM((CLUSTER, PAIR), narrow)
    slots = pltpu.VMEM((SLOTS, CLUSTER, TILE), narrow)
    sems = pltpu.SemaphoreType.DMA((SLOTS,))

    def blocks(plan, extra=0):
        lead = () if plan.split else (plan.nodes,)
        return [(lead + (plan.cap + extra, PAIR), narrow)] * plan.blocks

    def specs(plan):
        return [WHOLE] * plan.blocks

    def after(value, *others):
        return lax.optimization_barrier((value,) + others)[0]

    def head_swap(value, mask):
        pairs = [(index, index ^ mask) for index in range(HEAD_DEVICES)]
        return lax.ppermute(value, "head", pairs)

    def gather_heads(value, beside=None):
        far = head_swap(value, 2)
        turned = far if beside is None else after(far, beside)
        return [value, head_swap(value, 1), far, head_swap(turned, 1)]

    def swap(plan, wires):
        if not plan.split:
            return [lax.all_to_all(wires[0], "node", split_axis=0, concat_axis=0, tiled=True)]
        arrived = list(wires)
        for index in range(1, plan.nodes):
            pairs = [(node, node ^ plan.masks[index]) for node in range(plan.nodes)]
            arrived[index] = lax.ppermute(wires[index], "node", pairs)
        return arrived

    named = jnp.arange(plan.total, dtype=jnp.int32)[:, None] == cluster_ids[None, :]
    hist = jnp.sum(named, axis=1, dtype=jnp.int32)
    column = lax.axis_index("head").astype(jnp.int32)

    cotangents = [cotangent] + [head_swap(cotangent, mask) for mask in (1, 2, 3)]
    *wires, pos = call(
        pack_first_kernel, plan, "pack_queries_keys",
        blocks(plan, NOTE) + [((1, rows), jnp.int32)], specs(plan) + [WHOLE],
        [SCALARS, SCALARS, WHOLE, WHOLE, WHOLE], [starts, ordered], 2 * 10**9,
        (hist, me, cluster_ids.reshape(1, rows), queries, key_rows),
    )
    query_wires = swap(plan, wires)
    wires = call(
        pack_second_kernel, value_plan, "pack_values_grads", blocks(value_plan), specs(value_plan),
        [SCALARS] * 3 + [WHOLE] * (3 + HEAD_DEVICES),
        [starts, ordered, pltpu.VMEM((HEAD_DEVICES * width, rows), narrow)], 2 * 10**9,
        [hist, me, column.reshape(1), pos, value_rows, out_weight] + cotangents,
    )
    value_wires = swap(value_plan, wires)
    query_wires = [after(query_wires[0], wires[0])] + query_wires[1:]

    unit_rows_shape = ((plan.units, CLUSTER, PAIR), narrow)
    unit_keys_shape = ((plan.units, HEAD_DIM, CLUSTER), narrow)
    tiles_shape = ((plan.tiles + SPACE, CLUSTER, TILE), narrow)
    table_shape = (plan.nodes, PAIR)
    table, kept_queries, kept_keys, weights = call(
        weights_kernel, plan, "weights",
        [(table_shape, jnp.int32), unit_rows_shape, unit_keys_shape, tiles_shape],
        [SCALARS, WHOLE, WHOLE, APART], specs(plan),
        [pltpu.VMEM(table_shape, jnp.int32), stage, held, unit_counts, unit_block, unit_block,
         pltpu.SemaphoreType.DMA, slots, sems], 10 * 10**9,
        query_wires, UNIT_LIMIT,
    )
    all_weight = gather_heads(after(out_weight, kept_keys))
    *first_wires, dscores, kept_grads, counted = call(
        queries_kernel, (value_plan, first_plan), "attention_and_grad_queries",
        blocks(first_plan) + [tiles_shape, unit_rows_shape, ((plan.units,), jnp.int32)],
        specs(first_plan) + [APART, WHOLE, SCALARS],
        [SCALARS] * 2 + specs(value_plan) + [WHOLE, APART],
        [stage, held, unit_counts, unit_block, pltpu.VMEM((PAIR, CLUSTER), narrow), held, slots,
         sems, slots, sems], 10 * 10**9,
        [table, me] + value_wires + [kept_keys, weights], UNIT_LIMIT,
    )
    counted = after(counted, *all_weight[1:3])
    second_wires = call(
        keys_kernel, second_plan, "grad_keys_and_grad_values",
        blocks(second_plan), specs(second_plan),
        [SCALARS, SCALARS, SCALARS, WHOLE, WHOLE, APART, APART],
        [stage, held, pltpu.VMEM((CLUSTER, PAIR), jnp.float32), slots, slots, sems, sems],
        10 * 10**9,
        [table, me, counted, kept_queries, kept_grads, weights, dscores], UNIT_LIMIT,
    )

    def unpack(plan, wires, name):
        return call(
            unpack_kernel, plan, name, [home_shape, home_shape], [WHOLE, WHOLE],
            [SCALARS, SCALARS, WHOLE] + specs(plan),
            [starts, pltpu.VMEM((plan.heads, rows, PAIR), narrow)], 2 * 10**9,
            [hist, me, pos] + wires,
        )

    first_back = swap(first_plan, first_wires)
    second_back = swap(second_plan, second_wires)
    first_back = [after(first_back[0], second_wires[0])] + first_back[1:]
    attention, grad_queries = unpack(first_plan, first_back, "unpack_attention_grad_queries")
    (output,) = call(
        project_kernel, plan, "project", [home_shape], [WHOLE],
        [SCALARS] + [WHOLE] * (2 * HEAD_DEVICES),
        [pltpu.VMEM((HEAD_DEVICES, width, width), narrow)], 10**9,
        [column.reshape(1)] + all_weight + gather_heads(attention),
    )
    second_back[0] = after(second_back[0], output)
    grad_keys, grad_values = unpack(second_plan, second_back, "unpack_grad_keys_grad_values")
    return (output, grad_queries, grad_keys, grad_values)


def solution(mesh):
    placed = (
        P("head", "node"),
        P("head", "node"),
        P("head", "node"),
        P("head", None),
        P("head", "node"),
        P("node"),
        P("node", None),
        P("node"),
    )
    return jax.shard_map(
        body,
        mesh=mesh,
        in_specs=placed,
        out_specs=(P("head", "node"), P("head", "node"), P("head", "node"), P("head", "node")),
        check_vma=False,
    )
```

```python
import functools
import math

import jax
import jax.numpy as jnp
from jax import lax
from jax.experimental import pallas as pl
from jax.experimental.pallas import tpu as pltpu
from jax.sharding import PartitionSpec as P

HEAD_DIM = 64
CLUSTER = 1024
PAIR = 2 * HEAD_DIM
TILE = 256
SPARE = 32
NOTE = 16
HEAD_DEVICES = 4
MASKS = (
    (1, 7, 6, 5, 4, 2, 3),
    (1, 2, 7, 6, 5, 4, 3),
    (),
    (),
)
PAIRED_NODES = 8
UNIT_LIMIT = 46
SPACE = 16
SLOTS = 4
masked_score = -1e30

NT = (((1,), (1,)), ((), ()))
NN = (((1,), (0,)), ((), ()))
TN = (((0,), (0,)), ((), ()))


def dot(left, right, dims=NN):
    return lax.dot_general(left, right, dims, preferred_element_type=jnp.float32)


class Plan:
    def __init__(self, nodes, rows, width, clusters, masks):
        self.nodes = nodes
        self.rows = rows
        self.width = width
        self.heads = width // HEAD_DIM
        self.clusters = clusters
        self.total = nodes * clusters
        self.depth = 2 * rows // nodes
        self.half = self.depth // 2
        large = min(self.heads, nodes // 4)
        self.cap = large * self.depth + (self.heads - large) * self.half
        self.shift = tuple(3 * head % nodes for head in range(self.heads))
        self.units = self.heads * clusters
        self.tiles = self.units * (CLUSTER // TILE)
        self.paired = nodes == PAIRED_NODES
        self.split = self.paired and len(masks) > 0
        self.masks = (0,) + masks
        self.blocks = nodes if self.split else 1


def owner_rows(plan, hist, owner):
    return sum(hist[owner * plan.clusters + index, 0] for index in range(plan.clusters))


def each_block(plan, visit):
    if plan.split:
        for index in range(plan.nodes):
            visit(index)
    else:
        lax.fori_loop(0, plan.nodes, lambda index, carry: (visit(index), carry)[1], 0)


def block_of(plan, blocks, index):
    return blocks[index] if plan.split else blocks[0].at[index]


def partner(plan, me, index):
    return jnp.bitwise_xor(me, plan.masks[index]) if plan.split else index


def each_chunk(plan, hist, me, starts, visit):
    def begin(owner, at):
        starts[owner] = at
        return at + owner_rows(plan, hist, owner) // plan.half

    lax.fori_loop(0, plan.nodes, begin, jnp.int32(0))

    def block(number):
        dest = partner(plan, me, number)
        slot = jnp.int32(0)
        for head in range(plan.heads):
            owner = lax.rem(dest + plan.shift[head], plan.nodes)
            row = starts[owner]
            count = owner_rows(plan, hist, owner) // plan.half
            for index in range(2):

                @pl.when(index < count)
                def _(slot=slot, head=head, row=row, index=index):
                    visit(number, slot + index, head, row + index)

            slot = slot + count

    each_block(plan, block)


def chunk_rows(plan, index):
    return pl.ds(pl.multiple_of(index * plan.half, plan.half), plan.half)


def spread(plan, pos, first, second, hist, me, starts, ordered, wires):
    parts = []
    for head in range(plan.heads):
        span = slice(head * HEAD_DIM, (head + 1) * HEAD_DIM)
        parts += [first[span, :], second[span, :]]
    source = jnp.concatenate(parts, axis=0)
    for at in range(0, plan.rows, TILE):
        row = lax.broadcasted_iota(jnp.int32, (TILE, plan.rows), 0) + at
        pick = (row == pos).astype(jnp.bfloat16)
        ordered[at : at + TILE, :] = dot(pick, source, NT).astype(jnp.bfloat16)

    def clear(number):
        block = block_of(plan, wires, number)
        block[...] = jnp.zeros(block.shape, block.dtype)

    each_block(plan, clear)

    def visit(number, slot, head, row):
        block_of(plan, wires, number)[chunk_rows(plan, slot), :] = ordered[
            chunk_rows(plan, row), head * PAIR : (head + 1) * PAIR
        ]

    each_chunk(plan, hist, me, starts, visit)


def pack_first_kernel(plan, me, ids, queries, keys, *refs):
    wires, refs = refs[: plan.blocks], refs[plan.blocks :]
    pos_out, hist, starts, ordered, counted, hist_sem = refs
    rows = plan.rows
    cluster = lax.broadcasted_iota(jnp.int32, (plan.total, rows), 0)
    named = (cluster == ids[...]).astype(jnp.float32)
    count = jnp.sum(named, axis=1, keepdims=True).astype(jnp.int32)
    counted[...] = jnp.broadcast_to(count, (plan.total, PAIR))
    hist_copy = pltpu.make_async_copy(counted, hist, hist_sem)
    hist_copy.start()
    rank = ids[...] * rows + lax.broadcasted_iota(jnp.int32, (1, rows), 1)
    rank = rank.astype(jnp.float32)
    column = jnp.broadcast_to(rank, (128, rows)).T
    parts = []
    for at in range(0, rows, 128):
        below = (column < rank[:, at : at + 128]).astype(jnp.float32)
        parts.append(jnp.sum(below, axis=0, keepdims=True))
    pos = jnp.concatenate(parts, axis=1).astype(jnp.int32)
    pos_out[...] = pos
    hist_copy.wait()
    spread(plan, pos, queries[...], keys[...], hist, me[0], starts, ordered, wires)
    lane = lax.broadcasted_iota(jnp.int32, (NOTE, PAIR), 1)

    def note(number):
        dest = partner(plan, me[0], number)
        counts = jnp.zeros((NOTE, PAIR), jnp.int32)
        for head in range(plan.heads):
            owner = lax.rem(dest + plan.shift[head], plan.nodes)
            for cluster in range(plan.clusters):
                unit = head * plan.clusters + cluster
                count = hist[owner * plan.clusters + cluster, 0]
                counts = jnp.where(lane == unit, count, counts)
        block_of(plan, wires, number)[plan.cap :, :] = counts.astype(jnp.float32).astype(
            jnp.bfloat16
        )

    each_block(plan, note)


def pack_second_kernel(plan, hist, me, column, pos, values, weight, *refs):
    cotangents, refs = refs[:HEAD_DEVICES], refs[HEAD_DEVICES:]
    wires, (starts, ordered, gathered) = refs[: plan.blocks], refs[plan.blocks :]
    for mask in range(HEAD_DEVICES):
        place = jnp.bitwise_xor(column[0], mask) * plan.width
        span = pl.ds(pl.multiple_of(place, plan.width), plan.width)
        gathered[span, :] = cotangents[mask][...]
    grad_in = dot(weight[...], gathered[...]).astype(jnp.bfloat16)
    spread(plan, pos[...], values[...], grad_in, hist, me[0], starts, ordered, wires)


def project_kernel(plan, column, *refs):
    weights, refs = refs[:HEAD_DEVICES], refs[HEAD_DEVICES:]
    attentions, (out, piece) = refs[:HEAD_DEVICES], refs[HEAD_DEVICES:]
    for index in range(HEAD_DEVICES):

        @pl.when(column[0] == index)
        def _(index=index):
            start = index * plan.width
            for mask in range(HEAD_DEVICES):
                piece[mask] = weights[mask][:, start : start + plan.width]

    total = jnp.zeros((plan.width, plan.rows), jnp.float32)
    for mask in range(HEAD_DEVICES):
        total = total + dot(piece[mask], attentions[mask][...], (((0,), (0,)), ((), ())))
    out[...] = total.astype(jnp.bfloat16)


def unpack_kernel(plan, hist, me, pos, *refs):
    wires, (first, second, starts, ordered) = refs[: plan.blocks], refs[plan.blocks :]

    def visit(number, slot, head, row):
        ordered[head, chunk_rows(plan, row), :] = block_of(plan, wires, number)[
            chunk_rows(plan, slot), :
        ]

    each_chunk(plan, hist, me[0], starts, visit)
    source = jnp.concatenate([ordered[head] for head in range(plan.heads)], axis=1)
    for at in range(0, plan.rows, TILE):
        row = lax.broadcasted_iota(jnp.int32, (plan.rows, TILE), 0)
        pick = (row == pos[:, at : at + TILE]).astype(jnp.bfloat16)
        out = dot(source, pick, TN).astype(jnp.bfloat16)
        for head in range(plan.heads):
            span = slice(head * HEAD_DIM, (head + 1) * HEAD_DIM)
            first[span, at : at + TILE] = out[head * PAIR : head * PAIR + HEAD_DIM, :]
            second[span, at : at + TILE] = out[head * PAIR + HEAD_DIM : (head + 1) * PAIR, :]


def each_group(plan, table, me, visit):
    def source(line, block, places):
        at = block * (plan.cap + SPARE)
        after = []
        for unit in range(plan.units):
            count = table[line, unit]
            visit(unit, places[unit], at, count)
            at = at + count
            after.append(places[unit] + count)
        return tuple(after)

    places = (jnp.int32(0),) * plan.units
    if not plan.paired:
        return lax.fori_loop(0, plan.nodes, lambda at, places: source(at, at, places), places)
    for mask in range(plan.nodes):
        block = plan.masks.index(mask) if plan.split else jnp.bitwise_xor(me, mask)
        places = source(mask, block, places)
    return places


def stage_rows(plan, index):
    start = index * (plan.cap + SPARE)
    return pl.ds(start if plan.split else pl.multiple_of(start, NOTE), plan.cap)


def gather_units(plan, table, me, wires, stage, held, counts):
    def widen(index):
        block = block_of(plan, wires, index)
        stage[stage_rows(plan, index), :] = block[0 : plan.cap, :].astype(jnp.float32)

    each_block(plan, widen)

    def visit(unit, place, at, count):
        def step(index, carry):
            held[unit, pl.ds(place + index * SPARE, SPARE), :] = stage[
                pl.ds(at + index * SPARE, SPARE), :
            ]
            return carry

        lax.fori_loop(0, pl.cdiv(count, SPARE), step, 0)

    totals = each_group(plan, table, me, visit)
    for unit in range(plan.units):
        counts[unit] = totals[unit]


def scatter_units(plan, table, me, held, stage, wires):
    def visit(unit, place, at, count):
        def step(index, carry):
            stage[pl.ds(at + index * SPARE, SPARE), :] = held[
                unit, pl.ds(place + index * SPARE, SPARE), :
            ]
            return carry

        lax.fori_loop(0, pl.cdiv(count, SPARE), step, 0)

    each_group(plan, table, me, visit)

    def narrow(index):
        rows = stage[stage_rows(plan, index), :].astype(jnp.bfloat16)
        block_of(plan, wires, index)[...] = rows

    each_block(plan, narrow)


def unit_rows(held, unit, count):
    row = lax.broadcasted_iota(jnp.int32, (CLUSTER, PAIR), 0)
    return jnp.where(row < count, held[unit, 0:CLUSTER, :], 0.0)


def tile_steps(plan, counts):
    return sum(pl.cdiv(counts[unit], TILE) for unit in range(plan.units))


class Tiles:
    def __init__(self, array, slots, sems):
        self.array, self.slots, self.sems = array, slots, sems

    def slot(self, step):
        return lax.rem(step, SLOTS)

    def fetch(self, step):
        at = self.slot(step)
        return pltpu.make_async_copy(self.array.at[step], self.slots.at[at], self.sems.at[at])

    def begin(self, steps):
        for step in range(SLOTS - 1):

            @pl.when(step < steps)
            def _(step=step):
                self.fetch(step).start()

    def read(self, step, steps):
        @pl.when(step + SLOTS - 1 < steps)
        def _():
            self.fetch(step + SLOTS - 1).start()

        self.fetch(step).wait()
        return self.slots[self.slot(step)]

    def store(self, step):
        at = self.slot(step)
        return pltpu.make_async_copy(self.slots.at[at], self.array.at[step], self.sems.at[at])

    def write(self, step, value):
        @pl.when(step >= SLOTS)
        def _():
            self.store(step - SLOTS).wait()

        self.slots[self.slot(step)] = value
        self.store(step).start()

    def finish(self, steps):
        for back in range(SLOTS, 0, -1):

            @pl.when(steps >= back)
            def _(back=back):
                self.store(steps - back).wait()


def each_unit(plan, counts, visit):
    def one(unit, step):
        return lax.cond(counts[unit] > 0, lambda: visit(unit, step), lambda: step)

    lax.fori_loop(0, plan.units, one, jnp.int32(0))


def weights_kernel(plan, *refs):
    wires, refs = refs[: plan.blocks], refs[plan.blocks :]
    (table, queries, keys_t, weights, noted, stage, held, counts, query_aug, key_aug, table_sem,
     slots, sems) = refs
    out = Tiles(weights, slots, sems)

    def note(index):
        row = block_of(plan, wires, index)[plan.cap :, :].astype(jnp.float32)
        line = plan.masks[index] if plan.split else index
        noted[pl.ds(line, 1), :] = row[0:1, :].astype(jnp.int32)

    each_block(plan, note)
    table_copy = pltpu.make_async_copy(noted, table, table_sem)
    table_copy.start()
    table_copy.wait()
    gather_units(plan, table, None, wires, stage, held, counts)
    factor = math.log2(math.e) / math.sqrt(HEAD_DIM)
    lane = lax.broadcasted_iota(jnp.int32, (CLUSTER, PAIR), 1)
    row = lax.broadcasted_iota(jnp.int32, (CLUSTER, PAIR), 0)

    def one_unit(unit, step):
        count = counts[unit]
        both = unit_rows(held, unit, count)
        turned = pltpu.roll(both, HEAD_DIM, 1)
        queries[unit] = jnp.where(lane < HEAD_DIM, both, 0.0).astype(jnp.bfloat16)
        keys_t[unit] = turned.T[0:HEAD_DIM, :].astype(jnp.bfloat16)
        one = jnp.where(lane == HEAD_DIM, 1.0, 0.0)
        query_aug[...] = jnp.where(lane < HEAD_DIM, both, one).astype(jnp.bfloat16)
        outside = jnp.where(jnp.logical_and(lane == HEAD_DIM, row >= count), masked_score, 0.0)
        key_aug[...] = jnp.where(lane < HEAD_DIM, turned, outside).astype(jnp.bfloat16)

        def one_tile(tile, step):
            part = query_aug[pl.ds(pl.multiple_of(tile * TILE, TILE), TILE), :]
            scores = dot(key_aug[...], part, NT)
            raised = jnp.exp2((scores - jnp.max(scores, axis=0, keepdims=True)) * factor)
            share = 1.0 / jnp.sum(raised, axis=0, keepdims=True)
            out.write(step, (raised * share).astype(jnp.bfloat16))
            return step + 1

        return lax.fori_loop(0, pl.cdiv(count, TILE), one_tile, step)

    each_unit(plan, counts, one_unit)
    out.finish(tile_steps(plan, counts))


def attention_kernel(plans, table, me, *refs):
    plan, plan_out = plans
    wires, refs = refs[: plan.blocks], refs[plan.blocks :]
    weights = refs[0]
    wires_out, refs = refs[1 : 1 + plan_out.blocks], refs[1 + plan_out.blocks :]
    (kept, deltas, counts_out, stage, held, counts, grad_rows, both_t, held_out, total, slots,
     sems) = refs
    tiles = Tiles(weights, slots, sems)
    gather_units(plan, table, me[0], wires, stage, held, counts)
    lane = lax.broadcasted_iota(jnp.int32, (CLUSTER, PAIR), 1)
    for unit in range(plan.units):
        counts_out[unit] = counts[unit]
    steps = tile_steps(plan, counts)
    tiles.begin(steps)

    def one_unit(unit, step):
        count = counts[unit]
        both = unit_rows(held, unit, count)
        kept[unit] = both.astype(jnp.bfloat16)
        grad_rows[...] = jnp.where(lane >= HEAD_DIM, both, 0.0).astype(jnp.bfloat16)
        both_t[...] = both.T.astype(jnp.bfloat16)
        total[...] = jnp.zeros_like(total)

        def one_tile(tile, step):
            span = pl.ds(pl.multiple_of(tile * TILE, TILE), TILE)
            held_weights = tiles.read(step, steps)
            mixed = dot(both_t[0:HEAD_DIM, :], held_weights).astype(jnp.bfloat16)
            mixed = mixed.astype(jnp.float32)
            grad_t = both_t[HEAD_DIM:PAIR, span].astype(jnp.float32)
            deltas[pl.ds(step, 1), :] = jnp.sum(grad_t * mixed, axis=0, keepdims=True)
            held_out[unit, span, :] = jnp.concatenate([mixed, jnp.zeros_like(mixed)], axis=0).T
            total[...] += dot(held_weights, grad_rows[span, :])
            return step + 1

        step = lax.fori_loop(0, pl.cdiv(count, TILE), one_tile, step)
        held_out[unit, 0:CLUSTER, :] = jnp.where(
            lane < HEAD_DIM, held_out[unit, 0:CLUSTER, :], total[...]
        )
        return step

    each_unit(plan, counts, one_unit)
    scatter_units(plan_out, table, me[0], held_out, stage, wires_out)


def scores_kernel(plan, table, me, counts, queries, keys_t, kept, deltas, weights, *refs):
    wires_out, refs = refs[: plan.blocks], refs[plan.blocks :]
    stage, held_out, total, grad_rows, slots, sems = refs
    steps = tile_steps(plan, counts)
    tiles = Tiles(weights, slots, sems)
    tiles.begin(steps)
    scale = 1.0 / math.sqrt(HEAD_DIM)
    lane = lax.broadcasted_iota(jnp.int32, (CLUSTER, PAIR), 1)

    def one_unit(unit, step):
        turned = pltpu.roll(kept[unit].astype(jnp.float32), HEAD_DIM, 1)
        grad_rows[...] = jnp.where(lane < HEAD_DIM, turned, 0.0).astype(jnp.bfloat16)
        total[...] = jnp.zeros_like(total)

        def one_tile(tile, step):
            span = pl.ds(pl.multiple_of(tile * TILE, TILE), TILE)
            held_weights = tiles.read(step, steps).astype(jnp.float32)
            dweights = dot(kept[unit], grad_rows[span, :], NT)
            delta = deltas[pl.ds(step, 1), :]
            dscores = (held_weights * (dweights - delta)).astype(jnp.bfloat16)
            grad_query = dot(keys_t[unit], dscores) * scale
            held_out[unit, span, :] = jnp.concatenate(
                [jnp.zeros_like(grad_query), grad_query], axis=0
            ).T
            total[...] += dot(dscores, queries[unit, span, :])
            return step + 1

        step = lax.fori_loop(0, pl.cdiv(counts[unit], TILE), one_tile, step)
        held_out[unit, 0:CLUSTER, :] = jnp.where(
            lane < HEAD_DIM, total[...] * scale, held_out[unit, 0:CLUSTER, :]
        )
        return step

    each_unit(plan, counts, one_unit)
    scatter_units(plan, table, me[0], held_out, stage, wires_out)


SCALARS = pl.BlockSpec(memory_space=pltpu.SMEM)
WHOLE = pl.BlockSpec(memory_space=pltpu.VMEM)
APART = pl.BlockSpec(memory_space=pltpu.HBM)


def call(kernel, plan, name, outs, out_specs, in_specs, scratch, flops, args, limit=56):
    shapes = [jax.ShapeDtypeStruct(shape, dtype) for shape, dtype in outs]
    moved = sum(math.prod(shape) * jnp.dtype(dtype).itemsize for shape, dtype in outs)
    return pl.pallas_call(
        functools.partial(kernel, plan),
        out_shape=shapes,
        in_specs=in_specs,
        out_specs=out_specs,
        scratch_shapes=scratch,
        compiler_params=pltpu.CompilerParams(vmem_limit_bytes=limit * 1024 * 1024),
        cost_estimate=pl.CostEstimate(flops=flops, bytes_accessed=2 * moved, transcendentals=0),
        name=name,
    )(*args)


def body(queries, key_rows, value_rows, out_weight, cotangent, cluster_ids, members, counts):
    nodes = lax.axis_size("node")
    width, rows = queries.shape
    query_plan, value_plan, first_plan, second_plan = [
        Plan(nodes, rows, width, members.shape[0], masks) for masks in MASKS
    ]
    plan = query_plan
    me = lax.axis_index("node").astype(jnp.int32).reshape(1)
    narrow = jnp.bfloat16
    home_shape = ((width, rows), narrow)
    starts = pltpu.SMEM((plan.nodes,), jnp.int32)
    ordered = pltpu.VMEM((rows, plan.heads * PAIR), narrow)
    stage = pltpu.VMEM((plan.nodes * (plan.cap + SPARE), PAIR), jnp.float32)
    held = pltpu.VMEM((plan.units, CLUSTER + SPARE, PAIR), jnp.float32)
    unit_counts = pltpu.SMEM((plan.units,), jnp.int32)
    unit_block = pltpu.VMEM((CLUSTER, PAIR), narrow)
    slots = pltpu.VMEM((SLOTS, CLUSTER, TILE), narrow)
    sems = pltpu.SemaphoreType.DMA((SLOTS,))

    def blocks(plan, extra=0):
        lead = () if plan.split else (plan.nodes,)
        return [(lead + (plan.cap + extra, PAIR), narrow)] * plan.blocks

    def specs(plan):
        return [WHOLE] * plan.blocks

    def after(value, *others):
        return lax.optimization_barrier((value,) + others)[0]

    def head_swap(value, mask):
        pairs = [(index, index ^ mask) for index in range(HEAD_DEVICES)]
        return lax.ppermute(value, "head", pairs)

    def gather_heads(value, beside=None):
        far = head_swap(value, 2)
        turned = far if beside is None else after(far, beside)
        return [value, head_swap(value, 1), far, head_swap(turned, 1)]

    def swap(plan, wires):
        if not plan.split:
            return [lax.all_to_all(wires[0], "node", split_axis=0, concat_axis=0, tiled=True)]
        arrived = list(wires)
        for index in range(1, plan.nodes):
            pairs = [(node, node ^ plan.masks[index]) for node in range(plan.nodes)]
            arrived[index] = lax.ppermute(wires[index], "node", pairs)
        return arrived

    column = lax.axis_index("head").astype(jnp.int32)

    cotangents = [cotangent] + [head_swap(cotangent, mask) for mask in (1, 2, 3)]
    *wires, pos, hist = call(
        pack_first_kernel, plan, "pack_queries_keys",
        blocks(plan, NOTE) + [((1, rows), jnp.int32), ((plan.total, PAIR), jnp.int32)], specs(plan) + [WHOLE, SCALARS],
        [SCALARS, WHOLE, WHOLE, WHOLE],
        [starts, ordered, pltpu.VMEM((plan.total, PAIR), jnp.int32), pltpu.SemaphoreType.DMA],
        2 * 10**9,
        (me, cluster_ids.reshape(1, rows), queries, key_rows),
    )
    query_wires = swap(plan, wires)
    wires = call(
        pack_second_kernel, value_plan, "pack_values_grads", blocks(value_plan), specs(value_plan),
        [SCALARS] * 3 + [WHOLE] * (3 + HEAD_DEVICES),
        [starts, ordered, pltpu.VMEM((HEAD_DEVICES * width, rows), narrow)], 2 * 10**9,
        [hist, me, column.reshape(1), pos, value_rows, out_weight] + cotangents,
    )
    value_wires = swap(value_plan, wires)
    query_wires = [after(query_wires[0], wires[0])] + query_wires[1:]

    unit_rows_shape = ((plan.units, CLUSTER, PAIR), narrow)
    unit_keys_shape = ((plan.units, HEAD_DIM, CLUSTER), narrow)
    tiles_shape = ((plan.tiles + SPACE, CLUSTER, TILE), narrow)
    table_shape = (plan.nodes, PAIR)
    table, kept_queries, kept_keys, weights = call(
        weights_kernel, plan, "weights",
        [(table_shape, jnp.int32), unit_rows_shape, unit_keys_shape, tiles_shape],
        [SCALARS, WHOLE, WHOLE, APART], specs(plan),
        [pltpu.VMEM(table_shape, jnp.int32), stage, held, unit_counts, unit_block, unit_block,
         pltpu.SemaphoreType.DMA, slots, sems], 10 * 10**9,
        query_wires, UNIT_LIMIT,
    )
    all_weight = gather_heads(after(out_weight, kept_keys))
    unit_total = pltpu.VMEM((CLUSTER, PAIR), jnp.float32)
    *first_wires, kept, deltas, counted = call(
        attention_kernel, (value_plan, first_plan), "attention_and_grad_values",
        blocks(first_plan)
        + [unit_rows_shape, ((plan.tiles, TILE), jnp.float32), ((plan.units,), jnp.int32)],
        specs(first_plan) + [WHOLE, WHOLE, SCALARS],
        [SCALARS] * 2 + specs(value_plan) + [APART],
        [stage, held, unit_counts, unit_block, pltpu.VMEM((PAIR, CLUSTER), narrow), held,
         unit_total, slots, sems], 10 * 10**9,
        [table, me] + value_wires + [weights], UNIT_LIMIT,
    )
    counted = after(counted, *all_weight[1:3])
    second_wires = call(
        scores_kernel, second_plan, "grad_keys_and_grad_queries",
        blocks(second_plan), specs(second_plan), [SCALARS] * 3 + [WHOLE] * 4 + [APART],
        [stage, held, unit_total, unit_block, slots, sems], 10 * 10**9,
        [table, me, counted, kept_queries, kept_keys, kept, deltas, weights], UNIT_LIMIT,
    )

    def unpack(plan, wires, name):
        return call(
            unpack_kernel, plan, name, [home_shape, home_shape], [WHOLE, WHOLE],
            [SCALARS, SCALARS, WHOLE] + specs(plan),
            [starts, pltpu.VMEM((plan.heads, rows, PAIR), narrow)], 2 * 10**9,
            [hist, me, pos] + wires,
        )

    first_back = swap(first_plan, first_wires)
    second_back = swap(second_plan, second_wires)
    first_back = [after(first_back[0], second_wires[0])] + first_back[1:]
    attention, grad_values = unpack(first_plan, first_back, "unpack_attention_grad_values")
    (output,) = call(
        project_kernel, plan, "project", [home_shape], [WHOLE],
        [SCALARS] + [WHOLE] * (2 * HEAD_DEVICES),
        [pltpu.VMEM((HEAD_DEVICES, width, width), narrow)], 10**9,
        [column.reshape(1)] + all_weight + gather_heads(attention),
    )
    second_back[0] = after(second_back[0], output)
    grad_keys, grad_queries = unpack(second_plan, second_back, "unpack_grad_keys_grad_queries")
    return (output, grad_queries, grad_keys, grad_values)


def solution(mesh):
    placed = (
        P("head", "node"),
        P("head", "node"),
        P("head", "node"),
        P("head", None),
        P("head", "node"),
        P("node"),
        P("node", None),
        P("node"),
    )
    return jax.shard_map(
        body,
        mesh=mesh,
        in_specs=placed,
        out_specs=(P("head", "node"), P("head", "node"), P("head", "node"), P("head", "node")),
        check_vma=False,
    )
```
